128 devices in a mesh: seq: 32 (over z, x, core), head: 4 (over y).
Axes of the slice: x: 4, y: 4, z: 4, core: 2. Of those that a mesh axis runs over, the one named last changes fastest.
Arguments:
- tokens: bfloat16 [8192, 2048], P('seq'), may hold values from -6 to 6
- order: int32 [8192], P('seq'), may hold values from 0 to 8191, as said below
- doc_lengths: int32 [8], replicated, may hold values from 1 to 2048, 8192 in all
- w_query: bfloat16 [2048, 2048], P(None, 'head'), may hold values from -0.125 to 0.125
- w_key: bfloat16 [2048, 2048], P(None, 'head'), may hold values from -0.125 to 0.125
- w_value: bfloat16 [2048, 4096], P(None, 'head'), may hold values from -0.125 to 0.125
- w_zgate: bfloat16 [2048, 4096], P(None, 'head'), may hold values from -0.125 to 0.125
- w_beta: bfloat16 [2048, 32], P(None, 'head'), may hold values from -0.125 to 0.125
- w_alpha: bfloat16 [2048, 32], P(None, 'head'), may hold values from -0.125 to 0.125
- conv_query: bfloat16 [4, 2048], P(None, 'head'), may hold values from -3 to 3
- conv_key: bfloat16 [4, 2048], P(None, 'head'), may hold values from -3 to 3
- conv_value: bfloat16 [4, 4096], P(None, 'head'), may hold values from -3 to 3
- decay_log: float32 [32], P('head'), may hold values from -8.5 to -3.2
- decay_bias: float32 [32], P('head'), may hold values from -2 to 1
- norm_gain: float32 [128], replicated, may hold values from 0.5 to 1.5
- w_out: bfloat16 [4096, 2048], P('head'), may hold values from -0.09375 to 0.09375
Outputs:
- mixed: bfloat16 [8192, 2048], P('seq', 'head')
The draws below stay inside these ranges and needn't reach their ends.
Inputs may be any that keep to these rules, and one draw needn't show every extreme that they name: `order`: a permutation of the positions; each shard of 256 loader rows sends at most 16 rows to any one balanced shard, exactly 16 to some; every shard receives 256; the number sent from shard s to shard d depends only on (d - s) mod the shard count. `doc_lengths`: sum to 8192, one is exactly 2048.
All inputs are finite; a program needn't handle non-finite values.
Results may differ from the reference program's by a relative error of at most 0.017.
Values may be sent and summed in bfloat16 or wider, within the bound.
No kernel may reach another device: no remote copies, remote signals or barrier semaphores. Data moves between devices by JAX's collectives and lax.ppermute only.
A program may use at most 128 MiB of HBM per device.

```python
import math
import jax
import jax.numpy as jnp
import numpy as np
from jax import lax

D = 2048
HK = 16
HV = 32
HEAD_DIMENSION = 128
KERNEL = 4
TOK_DEV = 256
TOKENS = 8192
DOC_MOST = 2048
NDOC = 8
N_HEAD = 4


def draw_order(key, part):
    key = jax.random.fold_in(key, 11)
    key_offsets, key_sizes, key_source, key_target = jax.random.split(key, 4)
    shards = TOKENS // TOK_DEV
    base = TOK_DEV // shards
    shuffled = jax.random.permutation(key_offsets, shards)
    extra = jax.random.randint(key_sizes, (shards // 2,), 0, base + 1).astype(jnp.int32)
    extra = extra.at[0].set(base)
    change = jnp.zeros((shards,), jnp.int32).at[shuffled[0::2]].set(extra).at[shuffled[1::2]].set(-extra)
    counts = base + change
    upper = jnp.cumsum(counts).astype(jnp.int32)
    ranks = jnp.arange(TOK_DEV, dtype=jnp.int32)
    offsets = jnp.sum((ranks[:, None] >= upper[None, :]).astype(jnp.int32), axis=1)
    source_perm = jax.vmap(lambda single: jax.random.permutation(single, TOK_DEV))(jax.random.split(key_source, shards)).astype(jnp.int32)
    target_perm = jax.vmap(lambda single: jax.random.permutation(single, TOK_DEV))(jax.random.split(key_target, shards)).astype(jnp.int32)
    sources = jnp.arange(shards, dtype=jnp.int32)[:, None]
    targets = (sources + offsets[None, :]) % shards
    landing = targets * TOK_DEV + target_perm[targets, ranks[None, :]]
    anchor = sources * TOK_DEV + source_perm
    return jnp.zeros((TOKENS,), jnp.int32).at[anchor.reshape(-1)].set(landing.reshape(-1).astype(jnp.int32))


def draw_decay_log(key, part):
    key = jax.random.fold_in(key, 5)
    return jax.random.uniform(key, (HV,), jnp.float32, -8.5, -3.2)


def block_levels(own_key, shape, cuts, low, largest):
    loudness, own = 1.0, jax.random.fold_in(own_key, 6)
    for axis_at, shards_of in cuts:
        steps = jnp.exp(jax.random.uniform(jax.random.fold_in(own, axis_at), (shards_of,), jnp.float32, low / len(cuts), largest / len(cuts)))
        loudness = loudness * jnp.repeat(steps, shape[axis_at] // shards_of).reshape([-1 if axis == axis_at else 1 for axis in range(len(shape))])
    return loudness


def split_up(count, total, reach, lean):
    weights = [(1 << 20) // math.isqrt(standing ** lean) + 1 for standing in range(2, count + 1)]
    surplus, holding = total - reach - (count - 1), [1] * (count - 1)
    while surplus > 0:
        candidates = [i for i in range(count - 1) if holding[i] < reach]
        whole, left = sum([weights[i] for i in candidates]), surplus
        for i in candidates:
            addition = min(reach - holding[i], max(1, left * weights[i] // whole), surplus)
            holding[i] = holding[i] + addition
            surplus = surplus - addition
    return np.array([reach] + holding)


def ragged_sizes(key, count, total, bound, slope):
    if count == 2:
        one = jax.random.randint(key, (), max(1, total - bound), min(bound, total - 1) + 1)
        return jnp.stack([one, total - one])
    sizes = jnp.asarray(split_up(count, total, bound, slope), jnp.int32)
    pairs = (count - 1) // 2
    source_of, receiver = sizes[1:1 + 2 * pairs:2], sizes[2:2 + 2 * pairs:2]
    slack = jnp.minimum(source_of - 1, bound - receiver)
    moved = jax.random.randint(jax.random.fold_in(key, 1), (pairs,), 0, 1 << 20) % (slack + 1)
    sizes = sizes.at[1:1 + 2 * pairs:2].set(source_of - moved).at[2:2 + 2 * pairs:2].set(receiver + moved)
    return sizes[jax.random.permutation(jax.random.fold_in(key, 2), count)]


def scatter_about(stream_key, extent, width, reach, cuts=(), kind=jnp.bfloat16):
    level = block_levels(stream_key, extent, cuts, -0.22, 0.18) if cuts else 1.0
    array = jax.random.normal(stream_key, extent, jnp.float32) * width * level
    return jnp.minimum(jnp.maximum(array, -reach), reach).astype(kind)


def setup_inputs(seed: int = 0) -> dict:
    key_list = jax.random.split(jax.random.key(seed), 17)
    tokens = scatter_about(key_list[0], (TOKENS, D), 1.0, 6.0, ((0, 32),))
    order = draw_order(jax.random.fold_in(key_list[16], 71), 0)
    doc_lengths = ragged_sizes(key_list[2], NDOC, TOKENS, DOC_MOST, 2).astype(jnp.int32)
    w_query = scatter_about(key_list[3], (D, HK * HEAD_DIMENSION), D ** -0.5, 0.125, ((1, 4),))
    w_key = scatter_about(key_list[4], (D, HK * HEAD_DIMENSION), D ** -0.5, 0.125, ((1, 4),))
    w_value = scatter_about(key_list[5], (D, HV * HEAD_DIMENSION), D ** -0.5, 0.125, ((1, 4),))
    w_zgate = scatter_about(key_list[6], (D, HV * HEAD_DIMENSION), D ** -0.5, 0.125, ((1, 4),))
    w_beta = scatter_about(key_list[7], (D, HV), D ** -0.5, 0.125, ((1, 4),))
    w_alpha = scatter_about(key_list[8], (D, HV), D ** -0.5, 0.125, ((1, 4),))
    conv_query = scatter_about(key_list[9], (KERNEL, HK * HEAD_DIMENSION), 0.5, 3.0, ((1, 4),))
    conv_key = scatter_about(key_list[10], (KERNEL, HK * HEAD_DIMENSION), 0.5, 3.0, ((1, 4),))
    conv_value = scatter_about(key_list[11], (KERNEL, HV * HEAD_DIMENSION), 0.5, 3.0, ((1, 4),))
    decay_log = draw_decay_log(jax.random.fold_in(key_list[16], 71), 0)
    decay_bias = jnp.clip(-2.0 + 3.0 * jax.random.uniform(key_list[13], (HV,), jnp.float32) ** block_levels(key_list[13], (HV,), ((0, 4),), -0.2, 0.2), -2.0, 1.0)
    norm_gain = jnp.clip(1.0 + 0.1 * jax.random.normal(key_list[14], (HEAD_DIMENSION,), jnp.float32), 0.5, 1.5)
    w_out = scatter_about(key_list[15], (HV * HEAD_DIMENSION, D), (HV * HEAD_DIMENSION) ** -0.5, 0.09375, ((0, 4),))
    return {"tokens": tokens, "order": order, "doc_lengths": doc_lengths, "w_query": w_query, "w_key": w_key, "w_value": w_value, "w_zgate": w_zgate, "w_beta": w_beta, "w_alpha": w_alpha, "conv_query": conv_query, "conv_key": conv_key, "conv_value": conv_value, "decay_log": decay_log, "decay_bias": decay_bias, "norm_gain": norm_gain, "w_out": w_out}


largest_found = lax.Precision.HIGHEST

def segment_ids(positions, doc_lengths):
    doc_ends = jnp.cumsum(doc_lengths).astype(jnp.int32)
    return lax.optimization_barrier(jnp.sum((positions[:, None] >= doc_ends[None, :]).astype(jnp.int32), axis=1))

def causal_conv(extended, ext_segment, weights, segment):
    count = segment.shape[0]
    total = jnp.zeros((count, extended.shape[1]), jnp.float32)
    for offset in range(KERNEL):
        rows = extended[offset:offset + count].astype(jnp.float32)
        inside = (ext_segment[offset:offset + count] == segment)[:, None]
        total = total + jnp.where(inside, rows, 0.0) * weights[offset].astype(jnp.float32)
    return jax.nn.silu(total)

def unit_rows(values, heads, factor):
    shaped = values.reshape(values.shape[0], heads, -1)
    return shaped * lax.rsqrt(lax.optimization_barrier(jnp.sum(shaped * shaped, axis=-1, keepdims=True)) + 1e-06) * factor

def reference(tokens, order, doc_lengths, w_query, w_key, w_value, w_zgate, w_beta, w_alpha, conv_query, conv_key, conv_value, decay_log, decay_bias, norm_gain, w_out):
    count = tokens.shape[0]
    balanced = jnp.zeros_like(tokens).at[order].set(tokens)
    positions = jnp.arange(count, dtype=jnp.int32)
    segment = segment_ids(positions, doc_lengths)
    ext_segment = jnp.concatenate([jnp.full((KERNEL - 1,), -1, jnp.int32), segment])

    def project(weight):
        return jnp.dot(balanced, weight, preferred_element_type=jnp.float32).astype(jnp.bfloat16)

    def convolve(weight, kernel):
        projected = project(weight)
        extended = jnp.concatenate([jnp.zeros((KERNEL - 1, projected.shape[1]), jnp.bfloat16), projected], axis=0)
        return causal_conv(extended, ext_segment, kernel, segment)
    query = unit_rows(convolve(w_query, conv_query), HK, HEAD_DIMENSION ** (-0.5))
    keys = unit_rows(convolve(w_key, conv_key), HK, 1.0)
    values = convolve(w_value, conv_value).reshape(count, HV, HEAD_DIMENSION)
    zgate = project(w_zgate).astype(jnp.float32).reshape(count, HV, HEAD_DIMENSION)
    beta = jax.nn.sigmoid(jnp.dot(balanced, w_beta, preferred_element_type=jnp.float32))
    decay = -jnp.exp(decay_log) * jax.nn.softplus(jnp.dot(balanced, w_alpha, preferred_element_type=jnp.float32) + decay_bias)
    keep = jnp.concatenate([jnp.zeros((1,), jnp.float32), (segment[1:] == segment[:-1]).astype(jnp.float32)])
    repeat = HV // HK

    def advance(running_state, inputs):
        query_row, key_row, value_row, beta_row, decay_row, keep_flag = inputs
        complete_queries = jnp.repeat(query_row, repeat, axis=0)
        complete_keys = jnp.repeat(key_row, repeat, axis=0)
        running_state = running_state * (jnp.exp(decay_row) * keep_flag)[:, None, None]
        recurrent_memory = jnp.einsum('mtq,mt->mq', running_state, complete_keys, precision=largest_found)
        delta = (value_row - recurrent_memory) * beta_row[:, None]
        running_state = running_state + complete_keys[:, :, None] * delta[:, None, :]
        return (running_state, jnp.einsum('mtq,mt->mq', running_state, complete_queries, precision=largest_found))
    _, attended = lax.scan(advance, jnp.zeros((HV, HEAD_DIMENSION, HEAD_DIMENSION), jnp.float32), (query, keys, values, beta, decay, keep))
    normed = attended * lax.rsqrt(lax.optimization_barrier(jnp.mean(attended * attended, axis=-1, keepdims=True)) + 1e-06) * norm_gain * jax.nn.silu(zgate)
    gated = normed.astype(jnp.bfloat16).reshape(count, HV * HEAD_DIMENSION)
    group_width = HV * HEAD_DIMENSION // N_HEAD
    mixed = jnp.zeros((count, D), jnp.float32)
    for group in range(N_HEAD):
        lower = group * group_width
        partial_sum = jnp.dot(gated[:, lower:lower + group_width], w_out[lower:lower + group_width], preferred_element_type=jnp.float32).astype(jnp.bfloat16)
        mixed = mixed + lax.optimization_barrier(partial_sum).astype(jnp.float32)
    return mixed.astype(jnp.bfloat16)
```

```python
import jax
import jax.numpy as jnp
from jax import lax
from jax.experimental import pallas as pl
from jax.experimental.pallas import tpu as pltpu
from jax.sharding import PartitionSpec as P

HEAD = 128
KERNEL = 4
TAIL = 16
LANES = 128
VMEM = pl.BlockSpec(memory_space=pltpu.VMEM)
SMEM = pl.BlockSpec(memory_space=pltpu.SMEM)
ANY = pl.BlockSpec(memory_space=pl.ANY)
F32 = jnp.float32
BF16 = jnp.bfloat16
HIGHEST = lax.Precision.HIGHEST


def iota(shape, axis):
    return lax.broadcasted_iota(jnp.int32, shape, axis)


def dot(left, right, contract=((1,), (0,)), precision=None):
    return lax.dot_general(
        left, right, (contract, ((), ())), precision=precision, preferred_element_type=F32
    )


def params(mib):
    return pltpu.CompilerParams(vmem_limit_bytes=mib << 20)


def pack_kernel(shards, order_ref, tokens_ref, send_ref):
    rows, width = tokens_ref.shape
    slots = send_ref.shape[0]
    capacity = slots // shards
    order = order_ref[...]
    bits = rows.bit_length() - 1
    target = lax.shift_right_logical(order, jnp.full_like(order, bits))
    landing = lax.bitwise_and(order, jnp.full_like(order, rows - 1))
    marks = (iota((shards, rows), 0) == target).astype(F32)
    before = (iota((rows, rows), 0) < iota((rows, rows), 1)).astype(F32).astype(BF16)
    earlier = dot(marks.astype(BF16), before)
    slot = jnp.sum(earlier * marks, axis=0, keepdims=True).astype(jnp.int32)
    hit = (iota((slots, rows), 0) == target * capacity + slot).astype(F32)
    send_ref[:, :width] = dot(hit.astype(BF16), tokens_ref[...]).astype(BF16)
    spot = jnp.sum(hit * (landing + 1).astype(F32), axis=1, keepdims=True)
    send_ref[:, width:] = jnp.broadcast_to(spot, (slots, LANES)).astype(BF16)


def softplus(x):
    return jnp.maximum(x, 0.0) + jnp.log1p(jnp.exp(-jnp.abs(x)))


def project_kernel(
    got_ref,
    w_query,
    w_key,
    w_value,
    w_zgate,
    w_beta,
    w_alpha,
    decay_log,
    decay_bias,
    query_ref,
    key_ref,
    value_ref,
    zgate_ref,
    tail_ref,
    beta_ref,
    decay_ref,
    balanced_ref,
    query_buf,
    key_buf,
    value_buf,
    zgate_buf,
    sems,
):
    width, rows = balanced_ref.shape[1], balanced_ref.shape[0]
    slots = got_ref.shape[0]
    pairs = ((w_query, query_buf), (w_key, key_buf), (w_value, value_buf), (w_zgate, zgate_buf))
    copies = [pltpu.make_async_copy(w, buf, sems.at[i]) for i, (w, buf) in enumerate(pairs)]
    for copy in copies:
        copy.start()
    spot = got_ref[:, width : width + 1].astype(F32).astype(jnp.int32)
    hit = (spot == iota((slots, rows), 1) + 1).astype(F32)
    balanced_ref[...] = dot(hit.T.astype(BF16), got_ref[:, :width]).astype(BF16)
    balanced = balanced_ref[...]
    beta_ref[...] = jax.nn.sigmoid(dot(balanced, w_beta[...]))
    decay_ref[...] = -jnp.exp(decay_log[...]) * softplus(
        dot(balanced, w_alpha[...]) + decay_bias[...]
    )
    column = 0
    for copy, buf, out in zip(
        copies,
        (query_buf, key_buf, value_buf, zgate_buf),
        (query_ref, key_ref, value_ref, zgate_ref),
    ):
        copy.wait()
        count = out.shape[1]
        for start in range(0, count, 512):
            part = dot(balanced, buf[:, start : start + 512]).astype(BF16)
            out[:, start : start + 512] = part
            if out is not zgate_ref:
                tail_ref[:, column : column + 512] = part[rows - TAIL :]
                column += 512


def silu(x):
    return x / (1.0 + jnp.exp(-x))


def chunk_kernel(
    where_ref,
    lengths_ref,
    query_ref,
    key_ref,
    value_ref,
    tail_ref,
    taps_query,
    taps_key,
    taps_value,
    beta_ref,
    decay_ref,
    mine_ref,
    send_ref,
    base_ref,
    response_ref,
    system_ref,
    inverse_ref,
    queries,
    keys,
    values,
    mixing_ref,
    mask_ref,
):
    rows = query_ref.shape[0]
    first, core = where_ref[0], where_ref[1]
    heads = beta_ref.shape[1]
    key_heads = query_ref.shape[1] // HEAD

    ends, total = [], jnp.int32(0)
    for i in range(lengths_ref.shape[0]):
        total = total + lengths_ref[i]
        ends.append(total)

    def segments(position):
        count = jnp.zeros(position.shape, jnp.int32)
        for end in ends:
            count = count + (position >= end).astype(jnp.int32)
        return count

    position = first + iota((rows, 1), 0)
    segment = segments(position)
    segment_row = segments(first + iota((1, rows), 1))
    segment_before = segments(jnp.full((1, 1), first - 1, jnp.int32))
    same = [(segments(position - lag) == segment).astype(F32) for lag in range(KERNEL)]

    def convolve(projected, tail, taps):
        extended = jnp.concatenate([tail.astype(F32), projected.astype(F32)], axis=0)
        sums = None
        for lag in range(KERNEL):
            shifted = extended if lag == 0 else pltpu.roll(extended, lag, 0)
            tap = taps[KERNEL - 1 - lag : KERNEL - lag, :].astype(F32)
            term = shifted[TAIL:] * tap * same[lag]
            sums = term if sums is None else sums + term
        return silu(sums)

    def unit(x, factor):
        return x * (lax.rsqrt(jnp.sum(x * x, axis=-1, keepdims=True) + 1e-06) * factor)

    width = query_ref.shape[1]
    for h in range(key_heads):
        at = slice(h * HEAD, (h + 1) * HEAD)
        to = slice(width + h * HEAD, width + (h + 1) * HEAD)
        queries[h] = unit(
            convolve(query_ref[:, at], tail_ref[:, at], taps_query[:, at]), HEAD**-0.5
        ).astype(BF16)
        keys[h] = unit(convolve(key_ref[:, at], tail_ref[:, to], taps_key[:, at]), 1.0).astype(
            BF16
        )
    for h in range(heads):
        at = slice(h * HEAD, (h + 1) * HEAD)
        to = slice(2 * width + h * HEAD, 2 * width + (h + 1) * HEAD)
        values[h] = convolve(value_ref[:, at], tail_ref[:, to], taps_value[:, at]).astype(BF16)

    row, column = iota((rows, rows), 0), iota((rows, rows), 1)
    lower = (row >= column).astype(F32)
    cumulative = dot(lower, decay_ref[...], precision=HIGHEST)
    padded = jnp.concatenate([cumulative, jnp.zeros((rows, LANES - heads), F32)], axis=1)
    cumulative_row = padded.T
    inside = (row >= column) & (segment == segment_row)
    strict = (row > column).astype(F32)
    carries = (segment == segment_before).astype(F32)
    levels = []
    size = 1
    while size < rows:
        levels.append(size)
        block = lax.bitwise_and(
            (lax.bitwise_xor(row, column) < 2 * size).astype(jnp.int32),
            lax.bitwise_and(
                (lax.bitwise_and(row, size) != 0).astype(jnp.int32),
                (lax.bitwise_and(column, size) == 0).astype(jnp.int32),
            ),
        )
        mask_ref[len(levels) - 1] = block.astype(F32).astype(BF16)
        size *= 2
    unit_matrix = (row == column).astype(F32)

    for kh in range(key_heads):
        inner = dot(keys[kh], keys[kh], ((1,), (1,)))
        cross = dot(queries[kh], keys[kh], ((1,), (1,)))
        for h in range(kh * heads // key_heads, (kh + 1) * heads // key_heads):
            difference = cumulative[:, h : h + 1] - cumulative_row[h : h + 1, :]
            weights = jnp.where(inside, jnp.exp(jnp.where(inside, difference, 0.0)), 0.0)
            system = beta_ref[:, h : h + 1] * weights * inner * strict
            system_ref[h] = system.astype(BF16)
            mixing_ref[h] = (weights * cross).astype(BF16)
            inverse_ref[h] = (unit_matrix - system * mask_ref[0].astype(F32)).astype(BF16)
    for level in range(1, len(levels)):
        for h in range(heads):
            inverse = inverse_ref[h]
            part = dot(system_ref[h] * mask_ref[level], inverse).astype(BF16)
            inverse_ref[h] = (inverse.astype(F32) - dot(inverse, part)).astype(BF16)

    square = (iota((HEAD, HEAD), 0) == iota((HEAD, HEAD), 1)).astype(F32)
    half = heads // 2
    for h in range(heads):
        kh = h * key_heads // heads
        beta = beta_ref[:, h : h + 1]
        gain = cumulative[:, h : h + 1]
        carried = jnp.exp(gain) * carries
        key = keys[kh].astype(F32)
        right = jnp.concatenate(
            [(beta * values[h].astype(F32)).astype(BF16), (beta * carried * key).astype(BF16)],
            axis=1,
        )
        solved = dot(inverse_ref[h], right).astype(BF16)
        mixed = dot(mixing_ref[h], solved)
        at = slice(h * HEAD, (h + 1) * HEAD)
        base_ref[:, at] = mixed[:, :HEAD]
        response_ref[:, at] = (carried * queries[kh].astype(F32) - mixed[:, HEAD:]).astype(BF16)
        last_same = (segment == segment[rows - 1 : rows, :]).astype(F32)
        last = jnp.exp(gain[rows - 1 : rows, :] - gain) * last_same
        ended = dot((last * key).T.astype(BF16), solved)
        forward = ended[:, :HEAD].astype(BF16)
        transition = (carried[rows - 1 : rows, :] * square - ended[:, HEAD:]).astype(BF16)
        low = h < half
        ours = (core == 0) if low else (core == 1)
        local = h % half

        @pl.when(ours)
        def _():
            mine_ref[0, local] = transition
            mine_ref[1, local] = forward

        @pl.when(jnp.logical_not(ours))
        def _():
            send_ref[0, local] = transition
            send_ref[1, local] = forward


def chip_kernel(where_ref, mine_ref, other_ref, chip_ref):
    core = where_ref[1]

    def compose(early, late):
        for h in range(mine_ref.shape[1]):
            left = late[0, h]
            chip_ref[0, h] = dot(left, early[0, h]).astype(BF16)
            chip_ref[1, h] = (dot(left, early[1, h]) + late[1, h].astype(F32)).astype(BF16)

    @pl.when(core == 0)
    def _():
        compose(mine_ref, other_ref)

    @pl.when(core != 0)
    def _():
        compose(other_ref, mine_ref)


def pair_kernel(chip_ref, before_ref, pair_ref):
    for h in range(chip_ref.shape[1]):
        left = chip_ref[0, h]
        pair_ref[0, h] = dot(left, before_ref[0, h]).astype(BF16)
        pair_ref[1, h] = (dot(left, before_ref[1, h]) + chip_ref[1, h].astype(F32)).astype(BF16)


def enter_kernel(where_ref, near_ref, far_ref, mine_ref, other_ref, keep_ref, send_ref):
    core = where_ref[1]
    for h in range(far_ref.shape[0]):
        entering = dot(near_ref[0, h], far_ref[h]) + near_ref[1, h].astype(F32)
        entering_low = entering.astype(BF16)

        @pl.when(core == 0)
        def _():
            keep_ref[h] = entering_low
            later = dot(mine_ref[0, h], entering_low) + mine_ref[1, h].astype(F32)
            send_ref[h] = later.astype(BF16)

        @pl.when(core != 0)
        def _():
            send_ref[h] = entering_low
            later = dot(other_ref[0, h], entering_low) + other_ref[1, h].astype(F32)
            keep_ref[h] = later.astype(BF16)


def finish_kernel(
    where_ref,
    base_ref,
    response_ref,
    keep_ref,
    other_ref,
    zgate_ref,
    gain_ref,
    w_out,
    term_ref,
    gated_ref,
    state_ref,
):
    core = where_ref[1]
    half = keep_ref.shape[0]

    @pl.when(core == 0)
    def _():
        state_ref[:half] = keep_ref[...]
        state_ref[half:] = other_ref[...]

    @pl.when(core != 0)
    def _():
        state_ref[:half] = other_ref[...]
        state_ref[half:] = keep_ref[...]

    for h in range(2 * half):
        at = slice(h * HEAD, (h + 1) * HEAD)
        attended = base_ref[:, at] + dot(response_ref[:, at], state_ref[h])
        scale = lax.rsqrt(jnp.mean(attended * attended, axis=-1, keepdims=True) + 1e-06)
        gate = silu(zgate_ref[:, at].astype(F32))
        gated_ref[:, at] = (attended * scale * gain_ref[...] * gate).astype(BF16)
    gated = gated_ref[...]
    width = term_ref.shape[2]
    for part in range(term_ref.shape[0]):
        term_ref[part] = dot(gated, w_out[:, part * width : (part + 1) * width]).astype(BF16)


def out(*shape, dtype=BF16):
    return jax.ShapeDtypeStruct(shape, dtype)


def shifted(value, axis, steps):
    count = lax.axis_size(axis)
    return lax.ppermute(value, axis, [(at, at + steps) for at in range(count - steps)])


def turned(value, axis, steps):
    count = lax.axis_size(axis)
    return lax.ppermute(value, axis, [(at, (at + steps) % count) for at in range(count)])


def swapped(value, axis):
    count = lax.axis_size(axis)
    return lax.ppermute(value, axis, [(at, at ^ 1) for at in range(count)])


def local(
    tokens,
    order,
    doc_lengths,
    w_query,
    w_key,
    w_value,
    w_zgate,
    w_beta,
    w_alpha,
    conv_query,
    conv_key,
    conv_value,
    decay_log,
    decay_bias,
    norm_gain,
    w_out,
):
    rows, width = tokens.shape
    shards = lax.axis_size("seq")
    groups = lax.axis_size("head")
    capacity = 2 * rows // shards
    slots = shards * capacity
    qk, vw, heads = w_query.shape[1], w_value.shape[1], w_beta.shape[1]
    half = heads // 2
    index = lax.axis_index("seq")
    where = jnp.stack([index * rows, index % 2]).astype(jnp.int32)

    send = pl.pallas_call(
        lambda *refs: pack_kernel(shards, *refs),
        out_shape=out(slots, width + LANES),
        in_specs=[VMEM] * 2,
        out_specs=VMEM,
        compiler_params=params(24),
        name="pack",
    )(order.reshape(1, rows), tokens)
    got = lax.all_to_all(
        send.reshape(shards, capacity, width + LANES), "seq", split_axis=0, concat_axis=0, tiled=True
    ).reshape(slots, width + LANES)
    query, key, value, zgate, tail, beta, decay = pl.pallas_call(
        project_kernel,
        out_shape=(
            out(rows, qk),
            out(rows, qk),
            out(rows, vw),
            out(rows, vw),
            out(TAIL, 2 * qk + vw),
            out(rows, heads, dtype=F32),
            out(rows, heads, dtype=F32),
        ),
        in_specs=[VMEM] + [ANY] * 4 + [VMEM] * 4,
        out_specs=(VMEM,) * 7,
        scratch_shapes=[
            pltpu.VMEM((rows, width), BF16),
            pltpu.VMEM((width, qk), BF16),
            pltpu.VMEM((width, qk), BF16),
            pltpu.VMEM((width, vw), BF16),
            pltpu.VMEM((width, vw), BF16),
            pltpu.SemaphoreType.DMA((4,)),
        ],
        compiler_params=params(40),
        name="project",
    )(
        got,
        w_query,
        w_key,
        w_value,
        w_zgate,
        w_beta,
        w_alpha,
        decay_log.reshape(1, heads),
        decay_bias.reshape(1, heads),
    )
    tail_got = shifted(tail, "seq", 1)
    states = out(2, half, HEAD, HEAD)
    mine, sent, base, response = pl.pallas_call(
        chunk_kernel,
        out_shape=(states, states, out(rows, vw, dtype=F32), out(rows, vw)),
        in_specs=[SMEM] * 2 + [VMEM] * 9,
        out_specs=(VMEM,) * 4,
        scratch_shapes=[
            pltpu.VMEM((heads, rows, rows), BF16),
            pltpu.VMEM((heads, rows, rows), BF16),
            pltpu.VMEM((qk // HEAD, rows, HEAD), BF16),
            pltpu.VMEM((qk // HEAD, rows, HEAD), BF16),
            pltpu.VMEM((heads, rows, HEAD), BF16),
            pltpu.VMEM((heads, rows, rows), BF16),
            pltpu.VMEM((rows.bit_length() - 1, rows, rows), BF16),
        ],
        compiler_params=params(40),
        name="chunk",
    )(
        where,
        doc_lengths,
        query,
        key,
        value,
        tail_got,
        conv_query,
        conv_key,
        conv_value,
        beta,
        decay,
    )
    other = swapped(sent, "seq")
    chip = pl.pallas_call(
        chip_kernel,
        out_shape=states,
        in_specs=[SMEM, VMEM, VMEM],
        out_specs=VMEM,
        name="chip",
    )(where, mine, other)
    pair = pl.pallas_call(
        pair_kernel, out_shape=states, in_specs=[VMEM] * 2, out_specs=VMEM, name="pair"
    )(chip, shifted(chip, "seq", 2))
    near, far = shifted(pair, "seq", 2), shifted(pair[1], "seq", 6)
    state = out(half, HEAD, HEAD)
    keep, give = pl.pallas_call(
        enter_kernel,
        out_shape=(state, state),
        in_specs=[SMEM] + [VMEM] * 4,
        out_specs=(VMEM,) * 2,
        name="enter",
    )(where, near, far, mine, other)
    term = pl.pallas_call(
        finish_kernel,
        out_shape=out(groups, rows, width // groups),
        in_specs=[SMEM] + [VMEM] * 7,
        out_specs=VMEM,
        scratch_shapes=[pltpu.VMEM((rows, vw), BF16), pltpu.VMEM((heads, HEAD, HEAD), BF16)],
        compiler_params=params(32),
        name="finish",
    )(where, base, response, keep, swapped(give, "seq"), zgate, norm_gain.reshape(1, HEAD), w_out)
    here = lax.axis_index("head")
    mixed = lax.dynamic_index_in_dim(term, here, 0, keepdims=False).astype(F32)
    for steps in range(1, groups):
        leaving = lax.dynamic_index_in_dim(term, (here + steps) % groups, 0, keepdims=False)
        mixed = mixed + turned(leaving, "head", steps).astype(F32)
    return mixed.astype(BF16)


def solution(mesh):
    return jax.shard_map(
        local,
        mesh=mesh,
        in_specs=(
            P("seq", None),
            P("seq"),
            P(),
            P(None, "head"),
            P(None, "head"),
            P(None, "head"),
            P(None, "head"),
            P(None, "head"),
            P(None, "head"),
            P(None, "head"),
            P(None, "head"),
            P(None, "head"),
            P("head"),
            P("head"),
            P(),
            P("head", None),
        ),
        out_specs=P("seq", "head"),
        check_vma=False,
    )
```

```python
import jax
import jax.numpy as jnp
from jax import lax
from jax.experimental import pallas as pl
from jax.experimental.pallas import tpu as pltpu
from jax.sharding import PartitionSpec as P

HEAD = 128
KERNEL = 4
TAIL = 16
LANES = 128
FETCHES = 4
VMEM = pl.BlockSpec(memory_space=pltpu.VMEM)
SMEM = pl.BlockSpec(memory_space=pltpu.SMEM)
ANY = pl.BlockSpec(memory_space=pl.ANY)
F32 = jnp.float32
BF16 = jnp.bfloat16
HIGHEST = lax.Precision.HIGHEST


def iota(shape, axis):
    return lax.broadcasted_iota(jnp.int32, shape, axis)


def dot(left, right, contract=((1,), (0,)), precision=None):
    return lax.dot_general(
        left, right, (contract, ((), ())), precision=precision, preferred_element_type=F32
    )


def params(mib):
    return pltpu.CompilerParams(vmem_limit_bytes=mib << 20)


def pack_kernel(shards, order_ref, tokens_ref, send_ref):
    rows, width = tokens_ref.shape
    slots = send_ref.shape[0]
    capacity = slots // shards
    order = order_ref[...]
    bits = rows.bit_length() - 1
    target = lax.shift_right_logical(order, jnp.full_like(order, bits))
    landing = lax.bitwise_and(order, jnp.full_like(order, rows - 1))
    marks = (iota((shards, rows), 0) == target).astype(F32)
    before = (iota((rows, rows), 0) < iota((rows, rows), 1)).astype(F32).astype(BF16)
    earlier = dot(marks.astype(BF16), before)
    slot = jnp.sum(earlier * marks, axis=0, keepdims=True).astype(jnp.int32)
    hit = (iota((slots, rows), 0) == target * capacity + slot).astype(F32)
    send_ref[:, :width] = dot(hit.astype(BF16), tokens_ref[...]).astype(BF16)
    spot = jnp.sum(hit * (landing + 1).astype(F32), axis=1, keepdims=True)
    send_ref[:, width:] = jnp.broadcast_to(spot, (slots, LANES)).astype(BF16)


def softplus(x):
    return jnp.maximum(x, 0.0) + jnp.log1p(jnp.exp(-jnp.abs(x)))


def fetch_kernel(*refs):
    count = (len(refs) - 1) // 2
    copies = []
    for i, (source, target) in enumerate(zip(refs[:count], refs[count : 2 * count])):
        part = source.shape[0] // FETCHES
        for j in range(FETCHES):
            at = pl.ds(j * part, part)
            copies.append(
                pltpu.make_async_copy(source.at[at], target.at[at], refs[-1].at[i * FETCHES + j])
            )
    for copy in copies:
        copy.start()
    for copy in copies:
        copy.wait()


def project_kernel(
    got_ref,
    w_key,
    w_value,
    w_beta,
    w_alpha,
    decay_log,
    decay_bias,
    balanced_ref,
    key_ref,
    value_ref,
    tail_ref,
    beta_ref,
    decay_ref,
):
    rows, width = balanced_ref.shape
    slots = got_ref.shape[0]
    spot = got_ref[:, width : width + 1].astype(F32).astype(jnp.int32)
    hit = (spot == iota((slots, rows), 1) + 1).astype(F32).T.astype(BF16)
    for start in range(0, width, 512):
        part = slice(start, start + 512)
        balanced_ref[:, part] = dot(hit, got_ref[:, part]).astype(BF16)
    balanced = balanced_ref[...]
    across = ((1,), (1,))
    column = 0
    for weight, to in ((w_key, key_ref), (w_value, value_ref)):
        for start in range(0, to.shape[1], 512):
            part = dot(balanced, weight[:, start : start + 512]).astype(BF16)
            to[:, start : start + 512] = part
            tail_ref[:, column : column + 512] = part[rows - TAIL :]
            column += 512
    beta_ref[...] = jax.nn.sigmoid(dot(balanced, w_beta[...], across))
    decay_ref[...] = -jnp.exp(decay_log[...]) * softplus(
        dot(balanced, w_alpha[...], across) + decay_bias[...]
    )


def project_more_kernel(balanced_ref, w_query, w_zgate, query_ref, gate_ref, tail_ref):
    rows = balanced_ref.shape[0]
    balanced = balanced_ref[...]
    for weight, to in ((w_query, query_ref), (w_zgate, gate_ref)):
        for start in range(0, to.shape[1], 512):
            part = dot(balanced, weight[:, start : start + 512]).astype(BF16)
            to[:, start : start + 512] = part
            if to is query_ref:
                tail_ref[:, start : start + 512] = part[rows - TAIL :]


def silu(x):
    return x / (1.0 + jnp.exp(-x))


def document_ends(lengths_ref):
    ends, total = [], jnp.int32(0)
    for i in range(lengths_ref.shape[0]):
        total = total + lengths_ref[i]
        ends.append(total)
    return ends


def segments(position, ends):
    count = (position >= 0).astype(jnp.int32) - 1
    for end in ends:
        count = count + (position >= end).astype(jnp.int32)
    return count


def convolve(projected, tail, taps, same):
    extended = jnp.concatenate([tail.astype(F32), projected.astype(F32)], axis=0)
    sums = None
    for lag in range(KERNEL):
        rolled = extended if lag == 0 else pltpu.roll(extended, lag, 0)
        tap = taps[KERNEL - 1 - lag : KERNEL - lag, :].astype(F32)
        term = rolled[TAIL:] * tap
        if lag:
            term = term * same[lag - 1]
        sums = term if sums is None else sums + term
    return silu(sums)


def unit(x, factor):
    return x * (lax.rsqrt(jnp.sum(x * x, axis=-1, keepdims=True) + 1e-06) * factor)


def masks(first, ends, rows):
    position = first + iota((rows, 1), 0)
    segment = segments(position, ends)
    same = [
        (segments(position - lag, ends) == segment).astype(F32) for lag in range(1, KERNEL)
    ]
    inside = segment == segments(first + iota((1, rows), 1), ends)
    before = segments(jnp.full((1, 1), first - 1, jnp.int32), ends)
    carries = (segment == before).astype(F32)
    return segment, same, inside, carries


def cumulated(decay_ref):
    rows, heads = decay_ref.shape
    lower = (iota((rows, rows), 0) >= iota((rows, rows), 1)).astype(F32)
    down = dot(lower, decay_ref[...], precision=HIGHEST)
    padded = jnp.concatenate([down, jnp.zeros((rows, LANES - heads), F32)], axis=1)
    return down, padded.T


def between(down, across, h, inside):
    difference = down[:, h : h + 1] - across[h : h + 1, :]
    return jnp.where(inside, jnp.exp(jnp.where(inside, difference, 0.0)), 0.0)


def column_of(h):
    return slice(h * HEAD, (h + 1) * HEAD)


def chunk_kernel(
    where_ref,
    lengths_ref,
    key_ref,
    value_ref,
    tail_ref,
    taps_key,
    taps_value,
    beta_ref,
    decay_ref,
    mine_ref,
    send_ref,
    keys,
    solved_ref,
    system_ref,
    inverse_ref,
    mask_ref,
):
    rows = key_ref.shape[0]
    first, core = where_ref[0], where_ref[1]
    heads = beta_ref.shape[1]
    key_heads = key_ref.shape[1] // HEAD
    repeat = heads // key_heads
    width = key_ref.shape[1]
    segment, same, inside, carries = masks(first, document_ends(lengths_ref), rows)
    row, column = iota((rows, rows), 0), iota((rows, rows), 1)
    levels = rows.bit_length() - 1
    for level in range(levels):
        size = 1 << level
        apart = (lax.bitwise_xor(row, column) < 2 * size) & (
            lax.bitwise_and(row, size) > lax.bitwise_and(column, size)
        )
        mask_ref[level] = apart.astype(F32).astype(BF16)
    unit_matrix = (row == column).astype(F32)
    strict = inside & (row > column)
    down, across = cumulated(decay_ref)

    for kh in range(key_heads):
        at = column_of(kh)
        keys[kh] = unit(
            convolve(key_ref[:, at], tail_ref[:, at], taps_key[:, at], same), 1.0
        ).astype(BF16)
        inner = dot(keys[kh], keys[kh], ((1,), (1,)))
        for h in range(kh * repeat, (kh + 1) * repeat):
            system = beta_ref[:, h : h + 1] * inner * between(down, across, h, strict)
            system_ref[h] = system.astype(BF16)
            inverse_ref[h] = (unit_matrix - system * mask_ref[0].astype(F32)).astype(BF16)
    for level in range(1, levels):
        for h in range(heads):
            inverse = inverse_ref[h]
            part = dot(system_ref[h] * mask_ref[level], inverse).astype(BF16)
            inverse_ref[h] = (inverse.astype(F32) - dot(inverse, part)).astype(BF16)

    square = (iota((HEAD, HEAD), 0) == iota((HEAD, HEAD), 1)).astype(F32)
    half = heads // 2
    last_same = (segment == segment[rows - 1 : rows, :]).astype(F32)
    for h in range(heads):
        at, to = column_of(h), column_of(key_heads + h)
        beta = beta_ref[:, h : h + 1]
        gain = down[:, h : h + 1]
        carried = jnp.exp(gain) * carries
        key = keys[h // repeat].astype(F32)
        value = convolve(value_ref[:, at], tail_ref[:, to], taps_value[:, at], same)
        right = jnp.concatenate(
            [(beta * value).astype(BF16), (beta * carried * key).astype(BF16)], axis=1
        )
        solved = dot(inverse_ref[h], right).astype(BF16)
        solved_ref[h] = solved
        last = jnp.exp(gain[rows - 1 : rows, :] - gain) * last_same
        ended = dot((last * key).T.astype(BF16), solved)
        forward = ended[:, :HEAD].astype(BF16)
        transition = (carried[rows - 1 : rows, :] * square - ended[:, HEAD:]).astype(BF16)
        ours = (core == 0) if h < half else (core != 0)
        place = h % half

        @pl.when(ours)
        def _():
            mine_ref[0, place] = transition
            mine_ref[1, place] = forward

        @pl.when(jnp.logical_not(ours))
        def _():
            send_ref[0, place] = transition
            send_ref[1, place] = forward


def respond_kernel(
    where_ref,
    lengths_ref,
    query_ref,
    tail_ref,
    taps_query,
    decay_ref,
    keys,
    solved_ref,
    base_ref,
    response_ref,
):
    rows = query_ref.shape[0]
    heads = decay_ref.shape[1]
    key_heads = query_ref.shape[1] // HEAD
    repeat = heads // key_heads
    segment, same, inside, carries = masks(where_ref[0], document_ends(lengths_ref), rows)
    inside = inside & (iota((rows, rows), 0) >= iota((rows, rows), 1))
    down, across = cumulated(decay_ref)
    for kh in range(key_heads):
        at = column_of(kh)
        query = unit(
            convolve(query_ref[:, at], tail_ref[:, at], taps_query[:, at], same), HEAD**-0.5
        )
        cross = dot(query.astype(BF16), keys[kh], ((1,), (1,)))
        for h in range(kh * repeat, (kh + 1) * repeat):
            mixing = (between(down, across, h, inside) * cross).astype(BF16)
            mixed = dot(mixing, solved_ref[h])
            carried = jnp.exp(down[:, h : h + 1]) * carries
            base_ref[:, column_of(h)] = mixed[:, :HEAD]
            response_ref[:, column_of(h)] = (carried * query - mixed[:, HEAD:]).astype(BF16)


def gate_kernel(zgate_ref, gain_ref, gate_ref):
    for start in range(0, zgate_ref.shape[1], HEAD):
        at = slice(start, start + HEAD)
        gate_ref[:, at] = silu(zgate_ref[:, at].astype(F32)) * gain_ref[...]


def chip_kernel(where_ref, mine_ref, other_ref, chip_ref):
    core = where_ref[1]

    def compose(early, late):
        for h in range(mine_ref.shape[1]):
            left = late[0, h]
            chip_ref[0, h] = dot(left, early[0, h]).astype(BF16)
            chip_ref[1, h] = (dot(left, early[1, h]) + late[1, h].astype(F32)).astype(BF16)

    @pl.when(core == 0)
    def _():
        compose(mine_ref, other_ref)

    @pl.when(core != 0)
    def _():
        compose(other_ref, mine_ref)


def pair_kernel(chip_ref, before_ref, pair_ref, forward_ref):
    for h in range(chip_ref.shape[1]):
        left = chip_ref[0, h]
        pair_ref[0, h] = dot(left, before_ref[0, h]).astype(BF16)
        forward = (dot(left, before_ref[1, h]) + chip_ref[1, h].astype(F32)).astype(BF16)
        pair_ref[1, h] = forward
        forward_ref[h] = forward


def enter_kernel(where_ref, near_ref, far_ref, mine_ref, other_ref, keep_ref, send_ref):
    core = where_ref[1]
    for h in range(far_ref.shape[0]):
        entering = dot(near_ref[0, h], far_ref[h]) + near_ref[1, h].astype(F32)
        entering_low = entering.astype(BF16)

        @pl.when(core == 0)
        def _():
            keep_ref[h] = entering_low
            later = dot(mine_ref[0, h], entering_low) + mine_ref[1, h].astype(F32)
            send_ref[h] = later.astype(BF16)

        @pl.when(core != 0)
        def _():
            send_ref[h] = entering_low
            later = dot(other_ref[0, h], entering_low) + other_ref[1, h].astype(F32)
            keep_ref[h] = later.astype(BF16)


def finish_kernel(
    where_ref, base_ref, response_ref, keep_ref, other_ref, gate_ref, w_out, term_ref, gated_ref, state_ref
):
    core = where_ref[1]
    half = keep_ref.shape[0]

    @pl.when(core == 0)
    def _():
        state_ref[:half] = keep_ref[...]
        state_ref[half:] = other_ref[...]

    @pl.when(core != 0)
    def _():
        state_ref[:half] = other_ref[...]
        state_ref[half:] = keep_ref[...]

    for h in range(2 * half):
        at = column_of(h)
        attended = base_ref[:, at] + dot(response_ref[:, at], state_ref[h])
        scale = lax.rsqrt(jnp.mean(attended * attended, axis=-1, keepdims=True) + 1e-06)
        gated_ref[:, at] = (attended * scale * gate_ref[:, at]).astype(BF16)
    gated = gated_ref[...]
    width = term_ref.shape[2]
    for part in range(term_ref.shape[0]):
        term_ref[part] = dot(gated, w_out[:, part * width : (part + 1) * width]).astype(BF16)


def out(*shape, dtype=BF16):
    return jax.ShapeDtypeStruct(shape, dtype)


def turned(value, axis, steps):
    count = lax.axis_size(axis)
    return lax.ppermute(value, axis, [(at, (at + steps) % count) for at in range(count)])


def swapped(value, axis):
    count = lax.axis_size(axis)
    return lax.ppermute(value, axis, [(at, at ^ 1) for at in range(count)])


def after(value, *others):
    return lax.optimization_barrier((value, *others))[0]


def hbm(value):
    return pltpu.with_memory_space_constraint(value, pltpu.HBM)


def vmem(value):
    return pltpu.with_memory_space_constraint(value, pltpu.VMEM)


def call(kernel, name, outs, ins, mib, *, scratch=(), cost=2_000_000, inputs=None):
    single = not isinstance(outs, tuple)
    outs = (outs,) if single else outs
    got = pl.pallas_call(
        kernel,
        out_shape=outs,
        in_specs=[VMEM] * len(ins) if inputs is None else inputs,
        out_specs=(VMEM,) * len(outs),
        scratch_shapes=list(scratch),
        compiler_params=params(mib),
        cost_estimate=pl.CostEstimate(flops=0, bytes_accessed=cost, transcendentals=0),
        name=name,
    )(*ins)
    return got[0] if single else got


def local(
    tokens,
    order,
    doc_lengths,
    w_query,
    w_key,
    w_value,
    w_zgate,
    w_beta,
    w_alpha,
    conv_query,
    conv_key,
    conv_value,
    decay_log,
    decay_bias,
    norm_gain,
    w_out,
):
    rows, width = tokens.shape
    shards = lax.axis_size("seq")
    groups = lax.axis_size("head")
    capacity = 2 * rows // shards
    slots = shards * capacity
    qk, vw, heads = w_query.shape[1], w_value.shape[1], w_beta.shape[1]
    half, key_heads = heads // 2, qk // HEAD
    index = lax.axis_index("seq")
    where = jnp.stack([index * rows, index % 2]).astype(jnp.int32)

    send = call(
        lambda *refs: pack_kernel(shards, *refs),
        "pack",
        out(slots, width + LANES),
        (order.reshape(1, rows), hbm(tokens)),
        16,
    )
    weights = (w_key, w_value, w_query, w_zgate, w_out)
    weights = [hbm(after(weight, send)) for weight in weights]
    w_key, w_value, w_query, w_zgate, w_out = call(
        fetch_kernel,
        "fetch",
        tuple(pltpu.VMEM(weight.shape, weight.dtype) for weight in weights),
        weights,
        2,
        scratch=[pltpu.SemaphoreType.DMA((FETCHES * len(weights),))],
        inputs=[ANY] * len(weights),
        cost=20_000_000,
    )
    got = lax.all_to_all(
        send.reshape(shards, capacity, width + LANES), "seq", split_axis=0, concat_axis=0, tiled=True
    ).reshape(slots, width + LANES)
    balanced, key, value, tail, beta, decay = call(
        project_kernel,
        "project",
        (
            out(rows, width),
            out(rows, qk),
            out(rows, vw),
            out(TAIL, qk + vw),
            out(rows, heads, dtype=F32),
            out(rows, heads, dtype=F32),
        ),
        (
            vmem(got),
            vmem(w_key),
            vmem(w_value),
            w_beta.T,
            w_alpha.T,
            decay_log.reshape(1, heads),
            decay_bias.reshape(1, heads),
        ),
        16,
    )
    tail_got = turned(tail, "seq", 1)
    query, zgate, query_tail = call(
        project_more_kernel,
        "project_more",
        (out(rows, qk), out(rows, vw), out(TAIL, qk)),
        (balanced, vmem(w_query), vmem(w_zgate)),
        12,
    )
    tail_got, query = lax.optimization_barrier((tail_got, query))
    query_tail_got = turned(query_tail, "seq", 1)
    states = out(2, half, HEAD, HEAD)
    mine, sent, keys, solved = call(
        chunk_kernel,
        "chunk",
        (states, states, out(key_heads, rows, HEAD), out(heads, rows, 2 * HEAD)),
        (where, doc_lengths, key, value, tail_got, conv_key, conv_value, beta, decay),
        20,
        scratch=[
            pltpu.VMEM((heads, rows, rows), BF16),
            pltpu.VMEM((heads, rows, rows), BF16),
            pltpu.VMEM((rows.bit_length() - 1, rows, rows), BF16),
        ],
        inputs=[SMEM] * 2 + [VMEM] * 7,
    )
    other = swapped(sent, "seq")
    chip = call(
        chip_kernel, "chip", states, (where, mine, other), 4, inputs=[SMEM, VMEM, VMEM]
    )
    before = turned(chip, "seq", 2)
    base, response = call(
        respond_kernel,
        "respond",
        (out(rows, vw, dtype=F32), out(rows, vw)),
        (where, doc_lengths, after(query, chip), query_tail_got, conv_query, decay, keys, solved),
        16,
        inputs=[SMEM] * 2 + [VMEM] * 6,
        cost=16_000_000,
    )
    base, before = lax.optimization_barrier((base, before))
    pair_out = (states, out(half, HEAD, HEAD))
    pair, pair_forward = call(pair_kernel, "pair", pair_out, (chip, before), 4)
    near, far = turned(pair, "seq", 2), turned(pair_forward, "seq", 6)
    gate = call(
        gate_kernel,
        "gate",
        out(rows, vw, dtype=F32),
        (after(zgate, pair), norm_gain.reshape(1, HEAD)),
        8,
        cost=10_000_000,
    )
    gate, near, far = lax.optimization_barrier((gate, near, far))
    state = out(half, HEAD, HEAD)
    keep, give = call(
        enter_kernel,
        "enter",
        (state, state),
        (where, near, far, mine, other),
        4,
        inputs=[SMEM] + [VMEM] * 4,
    )
    term = call(
        finish_kernel,
        "finish",
        out(groups, rows, width // groups),
        (where, base, response, keep, swapped(give, "seq"), gate, vmem(w_out)),
        16,
        scratch=[pltpu.VMEM((rows, vw), BF16), pltpu.VMEM((heads, HEAD, HEAD), BF16)],
        inputs=[SMEM] + [VMEM] * 6,
    )
    here = lax.axis_index("head")
    mixed = lax.dynamic_index_in_dim(term, here, 0, keepdims=False).astype(F32)
    for steps in (2, 1, 3):
        leaving = lax.dynamic_index_in_dim(term, (here + steps) % groups, 0, keepdims=False)
        mixed = mixed + turned(leaving, "head", steps).astype(F32)
    return mixed.astype(BF16)


def solution(mesh):
    return jax.shard_map(
        local,
        mesh=mesh,
        in_specs=(
            P("seq", None),
            P("seq"),
            P(),
            P(None, "head"),
            P(None, "head"),
            P(None, "head"),
            P(None, "head"),
            P(None, "head"),
            P(None, "head"),
            P(None, "head"),
            P(None, "head"),
            P(None, "head"),
            P("head"),
            P("head"),
            P(),
            P("head", None),
        ),
        out_specs=P("seq", "head"),
        check_vma=False,
    )
```

```python
import jax
import jax.numpy as jnp
from jax import lax
from jax.experimental import pallas as pl
from jax.experimental.pallas import tpu as pltpu
from jax.sharding import PartitionSpec as P

HEAD = 128
KERNEL = 4
TAIL = 16
LANES = 128
FETCHES = 4
VMEM = pl.BlockSpec(memory_space=pltpu.VMEM)
SMEM = pl.BlockSpec(memory_space=pltpu.SMEM)
ANY = pl.BlockSpec(memory_space=pl.ANY)
F32 = jnp.float32
BF16 = jnp.bfloat16
HIGHEST = lax.Precision.HIGHEST


def iota(shape, axis):
    return lax.broadcasted_iota(jnp.int32, shape, axis)


def dot(left, right, contract=((1,), (0,)), precision=None):
    return lax.dot_general(
        left, right, (contract, ((), ())), precision=precision, preferred_element_type=F32
    )


def params(mib):
    return pltpu.CompilerParams(vmem_limit_bytes=mib << 20)


def pack_kernel(shards, order_ref, tokens_ref, send_ref, part_ref, sem):
    rows, width = part_ref.shape
    slots = send_ref.shape[0]
    capacity = slots // shards
    here = pl.multiple_of(lax.axis_index("head") * width, width)
    copy = pltpu.make_async_copy(tokens_ref.at[:, pl.ds(here, width)], part_ref, sem)
    copy.start()
    order = order_ref[...]
    bits = rows.bit_length() - 1
    target = lax.shift_right_logical(order, jnp.full_like(order, bits))
    landing = lax.bitwise_and(order, jnp.full_like(order, rows - 1))
    marks = (iota((shards, rows), 0) == target).astype(F32)
    before = (iota((rows, rows), 0) < iota((rows, rows), 1)).astype(F32).astype(BF16)
    earlier = dot(marks.astype(BF16), before)
    slot = jnp.sum(earlier * marks, axis=0, keepdims=True).astype(jnp.int32)
    hit = (iota((slots, rows), 0) == target * capacity + slot).astype(F32)
    spot = jnp.sum(hit * (landing + 1).astype(F32), axis=1, keepdims=True)
    send_ref[:, width:] = jnp.broadcast_to(spot, (slots, LANES)).astype(BF16)
    copy.wait()
    send_ref[:, :width] = dot(hit.astype(BF16), part_ref[...]).astype(BF16)


def place_kernel(got_ref, part_ref):
    rows, width = part_ref.shape
    slots = got_ref.shape[0]
    spot = got_ref[:, width : width + 1].astype(F32).astype(jnp.int32)
    hit = (spot == iota((slots, rows), 1) + 1).astype(F32).T.astype(BF16)
    part_ref[...] = dot(hit, got_ref[:, :width]).astype(BF16)


def softplus(x):
    return jnp.maximum(x, 0.0) + jnp.log1p(jnp.exp(-jnp.abs(x)))


def in_parts(source, target, sems, first):
    part = source.shape[0] // FETCHES
    return [
        pltpu.make_async_copy(
            source.at[pl.ds(j * part, part)], target.at[pl.ds(j * part, part)], sems.at[first + j]
        )
        for j in range(FETCHES)
    ]


def fetch_kernel(*refs):
    count = (len(refs) - 1) // 2
    copies = []
    for i, (source, target) in enumerate(zip(refs[:count], refs[count : 2 * count])):
        copies += in_parts(source, target, refs[-1], i * FETCHES)
    for copy in copies:
        copy.start()
    for copy in copies:
        copy.wait()


def project_kernel(
    part0_ref,
    part1_ref,
    part2_ref,
    part3_ref,
    w_query,
    w_key,
    w_value,
    w_beta,
    w_alpha,
    decay_log,
    decay_bias,
    balanced_ref,
    query_ref,
    key_ref,
    value_ref,
    tail_ref,
    beta_ref,
    decay_ref,
):
    rows = balanced_ref.shape[0]
    parts = (part0_ref, part1_ref, part2_ref, part3_ref)
    width = part0_ref.shape[1]
    here = lax.axis_index("head")
    for steps, part in enumerate(parts):
        at = lax.rem(here + len(parts) - steps, len(parts)) * width
        balanced_ref[:, pl.ds(pl.multiple_of(at, width), width)] = part[...]
    balanced = balanced_ref[...]
    across = ((1,), (1,))
    column = 0
    for weight, to in ((w_query, query_ref), (w_key, key_ref), (w_value, value_ref)):
        for start in range(0, to.shape[1], 512):
            part = dot(balanced, weight[:, start : start + 512]).astype(BF16)
            to[:, start : start + 512] = part
            tail_ref[:, column : column + 512] = part[rows - TAIL :]
            column += 512
    beta_ref[...] = jax.nn.sigmoid(dot(balanced, w_beta[...], across))
    decay_ref[...] = -jnp.exp(decay_log[...]) * softplus(
        dot(balanced, w_alpha[...], across) + decay_bias[...]
    )


def project_gate_kernel(balanced_ref, w_zgate, zgate_ref):
    balanced = balanced_ref[...]
    for start in range(0, zgate_ref.shape[1], 512):
        part = dot(balanced, w_zgate[:, start : start + 512])
        zgate_ref[:, start : start + 512] = part.astype(BF16)


def silu(x):
    return x / (1.0 + jnp.exp(-x))


def document_ends(lengths_ref):
    ends, total = [], jnp.int32(0)
    for i in range(lengths_ref.shape[0]):
        total = total + lengths_ref[i]
        ends.append(total)
    return ends


def segments(position, ends):
    count = (position >= 0).astype(jnp.int32) - 1
    for end in ends:
        count = count + (position >= end).astype(jnp.int32)
    return count


def convolve(projected, tail, taps, same):
    extended = jnp.concatenate([tail.astype(F32), projected.astype(F32)], axis=0)
    sums = None
    for lag in range(KERNEL):
        rolled = extended if lag == 0 else pltpu.roll(extended, lag, 0)
        tap = taps[KERNEL - 1 - lag : KERNEL - lag, :].astype(F32)
        term = rolled[TAIL:] * tap
        if lag:
            term = term * same[lag - 1]
        sums = term if sums is None else sums + term
    return silu(sums)


def unit(x, factor):
    return x * (lax.rsqrt(jnp.sum(x * x, axis=-1, keepdims=True) + 1e-06) * factor)


def masks(first, ends, rows):
    position = first + iota((rows, 1), 0)
    segment = segments(position, ends)
    same = [
        (segments(position - lag, ends) == segment).astype(F32) for lag in range(1, KERNEL)
    ]
    inside = segment == segments(first + iota((1, rows), 1), ends)
    before = segments(jnp.full((1, 1), first - 1, jnp.int32), ends)
    carries = (segment == before).astype(F32)
    return segment, same, inside, carries


def cumulated(decay_ref):
    rows, heads = decay_ref.shape
    lower = (iota((rows, rows), 0) >= iota((rows, rows), 1)).astype(F32)
    down = dot(lower, decay_ref[...], precision=HIGHEST)
    padded = jnp.concatenate([down, jnp.zeros((rows, LANES - heads), F32)], axis=1)
    return down, padded.T


def between(down, across, h, inside):
    difference = down[:, h : h + 1] - across[h : h + 1, :]
    return jnp.where(inside, jnp.exp(jnp.where(inside, difference, 0.0)), 0.0)


def my_core():
    return lax.rem(lax.axis_index("seq"), 2)


def column_of(h):
    return slice(h * HEAD, (h + 1) * HEAD)


def chunk_kernel(
    lengths_ref,
    key_ref,
    value_ref,
    tail_ref,
    taps_key,
    taps_value,
    beta_ref,
    decay_ref,
    mine_ref,
    send_ref,
    keys,
    solved_ref,
    system_ref,
    inverse_ref,
    mask_ref,
    states_ref,
    right_ref,
):
    rows = key_ref.shape[0]
    first, core = lax.axis_index("seq") * rows, my_core()
    heads = beta_ref.shape[1]
    key_heads = key_ref.shape[1] // HEAD
    repeat = heads // key_heads
    width = key_ref.shape[1]
    segment, same, inside, carries = masks(first, document_ends(lengths_ref), rows)
    row, column = iota((rows, rows), 0), iota((rows, rows), 1)
    levels = rows.bit_length() - 1
    for level in range(levels):
        size = 1 << level
        apart = (lax.bitwise_xor(row, column) < 2 * size) & (
            lax.bitwise_and(row, size) > lax.bitwise_and(column, size)
        )
        mask_ref[level] = apart.astype(F32).astype(BF16)
    unit_matrix = (row == column).astype(F32)
    strict = inside & (row > column)
    down, across = cumulated(decay_ref)

    for kh in range(key_heads):
        at = column_of(kh)
        keys[kh] = unit(
            convolve(key_ref[:, at], tail_ref[:, column_of(key_heads + kh)], taps_key[:, at], same), 1.0
        ).astype(BF16)
        inner = dot(keys[kh], keys[kh], ((1,), (1,)))
        for h in range(kh * repeat, (kh + 1) * repeat):
            system = beta_ref[:, h : h + 1] * inner * between(down, across, h, strict)
            system_ref[h] = system.astype(BF16)
            inverse_ref[h] = (unit_matrix - system * mask_ref[0].astype(F32)).astype(BF16)
    for h in range(heads):
        at, to = column_of(h), column_of(2 * key_heads + h)
        beta = beta_ref[:, h : h + 1]
        carried = jnp.exp(down[:, h : h + 1]) * carries
        value = convolve(value_ref[:, at], tail_ref[:, to], taps_value[:, at], same)
        right_ref[h, :, :HEAD] = (beta * value).astype(BF16)
        right_ref[h, :, HEAD:] = (beta * carried * keys[h // repeat].astype(F32)).astype(BF16)
    for level in range(1, levels):
        for h in range(heads):
            inverse = inverse_ref[h]
            part = dot(system_ref[h] * mask_ref[level], inverse).astype(BF16)
            inverse_ref[h] = (inverse.astype(F32) - dot(inverse, part)).astype(BF16)

    square = (iota((HEAD, HEAD), 0) == iota((HEAD, HEAD), 1)).astype(F32)
    half = heads // 2
    last_same = (segment == segment[rows - 1 : rows, :]).astype(F32)
    for h in range(heads):
        solved_ref[h] = dot(inverse_ref[h], right_ref[h]).astype(BF16)
    for h in range(heads):
        gain = down[:, h : h + 1]
        last = jnp.exp(gain[rows - 1 : rows, :] - gain) * last_same
        ended = dot((last * keys[h // repeat].astype(F32)).astype(BF16), solved_ref[h], ((0,), (0,)))
        carried = (jnp.exp(gain) * carries)[rows - 1 : rows, :]
        states_ref[0, h] = (carried * square - ended[:, HEAD:]).astype(BF16)
        states_ref[1, h] = ended[:, :HEAD].astype(BF16)

    @pl.when(core == 0)
    def _():
        mine_ref[...] = states_ref[:, :half]
        send_ref[...] = states_ref[:, half:]

    @pl.when(core != 0)
    def _():
        mine_ref[...] = states_ref[:, half:]
        send_ref[...] = states_ref[:, :half]


def chunk_scratch(heads, rows):
    return [
        pltpu.VMEM((heads, rows, rows), BF16),
        pltpu.VMEM((heads, rows, rows), BF16),
        pltpu.VMEM((rows.bit_length() - 1, rows, rows), BF16),
        pltpu.VMEM((2, heads, HEAD, HEAD), BF16),
        pltpu.VMEM((heads, rows, 2 * HEAD), BF16),
    ]


def respond_kernel(
    lengths_ref,
    query_ref,
    tail_ref,
    taps_query,
    decay_ref,
    keys,
    solved_ref,
    base_ref,
    response_ref,
):
    rows = query_ref.shape[0]
    heads = decay_ref.shape[1]
    key_heads = query_ref.shape[1] // HEAD
    repeat = heads // key_heads
    segment, same, inside, carries = masks(
        lax.axis_index("seq") * rows, document_ends(lengths_ref), rows
    )
    inside = inside & (iota((rows, rows), 0) >= iota((rows, rows), 1))
    down, across = cumulated(decay_ref)
    for kh in range(key_heads):
        at = column_of(kh)
        query = unit(
            convolve(query_ref[:, at], tail_ref[:, at], taps_query[:, at], same), HEAD**-0.5
        )
        cross = dot(query.astype(BF16), keys[kh], ((1,), (1,)))
        for h in range(kh * repeat, (kh + 1) * repeat):
            mixing = (between(down, across, h, inside) * cross).astype(BF16)
            mixed = dot(mixing, solved_ref[h])
            carried = jnp.exp(down[:, h : h + 1]) * carries
            base_ref[:, column_of(h)] = mixed[:, :HEAD]
            response_ref[:, column_of(h)] = (carried * query - mixed[:, HEAD:]).astype(BF16)


def gate_kernel(zgate_ref, gain_ref, w_out, gate_ref, out_ref, sems):
    copies = in_parts(w_out, out_ref, sems, 0)
    for copy in copies:
        copy.start()
    for start in range(0, zgate_ref.shape[1], HEAD):
        at = slice(start, start + HEAD)
        gate_ref[:, at] = silu(zgate_ref[:, at].astype(F32)) * gain_ref[...]
    for copy in copies:
        copy.wait()


def chip_kernel(mine_ref, other_ref, chip_ref):
    core = my_core()

    def compose(early, late):
        for h in range(mine_ref.shape[1]):
            left = late[0, h]
            chip_ref[0, h] = dot(left, early[0, h]).astype(BF16)
            chip_ref[1, h] = (dot(left, early[1, h]) + late[1, h].astype(F32)).astype(BF16)

    @pl.when(core == 0)
    def _():
        compose(mine_ref, other_ref)

    @pl.when(core != 0)
    def _():
        compose(other_ref, mine_ref)


def pair_kernel(chip_ref, before_ref, pair_ref, forward_ref):
    for h in range(chip_ref.shape[1]):
        left = chip_ref[0, h]
        pair_ref[0, h] = dot(left, before_ref[0, h]).astype(BF16)
        forward = (dot(left, before_ref[1, h]) + chip_ref[1, h].astype(F32)).astype(BF16)
        pair_ref[1, h] = forward
        forward_ref[h] = forward


def enter_kernel(near_ref, far_ref, mine_ref, other_ref, keep_ref, send_ref):
    core = my_core()

    def step(first_ref, early_ref, late_ref):
        heads = range(far_ref.shape[0])
        for h in heads:
            entering = dot(near_ref[0, h], far_ref[h]) + near_ref[1, h].astype(F32)
            early_ref[h] = entering.astype(BF16)
        for h in heads:
            later = dot(first_ref[0, h], early_ref[h]) + first_ref[1, h].astype(F32)
            late_ref[h] = later.astype(BF16)

    @pl.when(core == 0)
    def _():
        step(mine_ref, keep_ref, send_ref)

    @pl.when(core != 0)
    def _():
        step(other_ref, send_ref, keep_ref)


def finish_kernel(
    base_ref,
    response_ref,
    keep_ref,
    other_ref,
    gate_ref,
    w_out,
    term0_ref,
    term1_ref,
    term2_ref,
    term3_ref,
    gated_ref,
    state_ref,
):
    core = my_core()
    half = keep_ref.shape[0]

    @pl.when(core == 0)
    def _():
        state_ref[:half] = keep_ref[...]
        state_ref[half:] = other_ref[...]

    @pl.when(core != 0)
    def _():
        state_ref[:half] = other_ref[...]
        state_ref[half:] = keep_ref[...]

    for h in range(2 * half):
        at = column_of(h)
        attended = base_ref[:, at] + dot(response_ref[:, at], state_ref[h])
        scale = lax.rsqrt(jnp.mean(attended * attended, axis=-1, keepdims=True) + 1e-06)
        gated_ref[:, at] = (attended * scale * gate_ref[:, at]).astype(BF16)
    gated = gated_ref[...]
    terms = (term0_ref, term1_ref, term2_ref, term3_ref)
    width = term0_ref.shape[1]
    here = lax.axis_index("head")
    for steps, term in enumerate(terms):
        at = pl.multiple_of(lax.rem(here + steps, len(terms)) * width, width)
        term[...] = dot(gated, w_out[:, pl.ds(at, width)]).astype(BF16)


def out(*shape, dtype=BF16):
    return pltpu.VMEM(shape, dtype)


def turned(value, axis, steps):
    count = lax.axis_size(axis)
    return lax.ppermute(value, axis, [(at, (at + steps) % count) for at in range(count)])


def swapped(value, axis):
    count = lax.axis_size(axis)
    return lax.ppermute(value, axis, [(at, at ^ 1) for at in range(count)])


def after(value, *others):
    return lax.optimization_barrier((value, *others))[0]


def hbm(value):
    return pltpu.with_memory_space_constraint(value, pltpu.HBM)


def vmem(value):
    return pltpu.with_memory_space_constraint(value, pltpu.VMEM)


def call(kernel, name, outs, ins, mib, *, scratch=(), cost=2_000_000, inputs=None, specs=None):
    single = not isinstance(outs, tuple)
    outs = (outs,) if single else outs
    got = pl.pallas_call(
        kernel,
        out_shape=outs,
        in_specs=[VMEM] * len(ins) if inputs is None else inputs,
        out_specs=(VMEM,) * len(outs) if specs is None else specs,
        scratch_shapes=list(scratch),
        compiler_params=params(mib),
        cost_estimate=pl.CostEstimate(flops=0, bytes_accessed=cost, transcendentals=0),
        name=name,
    )(*ins)
    return got[0] if single else got


def local(
    tokens,
    order,
    doc_lengths,
    w_query,
    w_key,
    w_value,
    w_zgate,
    w_beta,
    w_alpha,
    conv_query,
    conv_key,
    conv_value,
    decay_log,
    decay_bias,
    norm_gain,
    w_out,
):
    rows, width = tokens.shape
    shards = lax.axis_size("seq")
    groups = lax.axis_size("head")
    capacity = 2 * rows // shards
    slots = shards * capacity
    qk, vw, heads = w_query.shape[1], w_value.shape[1], w_beta.shape[1]
    half, key_heads = heads // 2, qk // HEAD
    part = width // groups

    send = call(
        lambda *refs: pack_kernel(shards, *refs),
        "pack",
        pltpu.HBM((slots, part + LANES), BF16),
        (hbm(order.reshape(1, rows)), hbm(tokens)),
        8,
        scratch=[pltpu.VMEM((rows, part), BF16), pltpu.SemaphoreType.DMA],
        inputs=[VMEM, ANY],
    )
    got = lax.all_to_all(
        send.reshape(shards, capacity, part + LANES), "seq", split_axis=0, concat_axis=0, tiled=True
    ).reshape(slots, part + LANES)
    parts = [call(place_kernel, "place", out(rows, part), (got,), 4)]
    for steps in range(1, groups):
        parts.append(turned(parts[0], "head", steps))
    weights = [hbm(after(weight, parts[0])) for weight in (w_query, w_key, w_value, w_zgate)]
    fetched = call(
        fetch_kernel,
        "fetch",
        tuple(pltpu.VMEM(weight.shape, weight.dtype) for weight in weights),
        tuple(weights),
        2,
        scratch=[pltpu.SemaphoreType.DMA((FETCHES * len(weights),))],
        inputs=[ANY] * len(weights),
        specs=(ANY,) * len(weights),
        cost=20_000_000,
    )
    balanced, query, key, value, tail, beta, decay = call(
        project_kernel,
        "project",
        (
            out(rows, width),
            out(rows, qk),
            out(rows, qk),
            out(rows, vw),
            out(TAIL, 2 * qk + vw),
            out(rows, heads, dtype=F32),
            out(rows, heads, dtype=F32),
        ),
        (
            *parts,
            *[vmem(weight) for weight in fetched[:3]],
            w_beta.T,
            w_alpha.T,
            decay_log.reshape(1, heads),
            decay_bias.reshape(1, heads),
        ),
        8,
    )
    tail_got = turned(tail, "seq", 1)
    zgate = call(
        project_gate_kernel, "project_gate", out(rows, vw), (balanced, vmem(fetched[3])), 8
    )
    tail_got, zgate = lax.optimization_barrier((tail_got, zgate))
    states = out(2, half, HEAD, HEAD)
    mine, sent, keys, solved = call(
        chunk_kernel,
        "chunk",
        (states, states, out(key_heads, rows, HEAD), out(heads, rows, 2 * HEAD)),
        (doc_lengths, key, value, tail_got, conv_key, conv_value, beta, decay),
        16,
        scratch=chunk_scratch(heads, rows),
        inputs=[SMEM] + [VMEM] * 7,
    )
    other = swapped(sent, "seq")
    chip = call(chip_kernel, "chip", states, (mine, other), 4)
    before = turned(chip, "seq", 2)
    base, response = call(
        respond_kernel,
        "respond",
        (out(rows, vw, dtype=F32), out(rows, vw)),
        (doc_lengths, after(query, chip), tail_got, conv_query, decay, keys, solved),
        8,
        inputs=[SMEM] + [VMEM] * 6,
        cost=16_000_000,
    )
    base, before = lax.optimization_barrier((base, before))
    pair, pair_forward = call(
        pair_kernel, "pair", (states, out(half, HEAD, HEAD)), (chip, before), 4
    )
    near, far = turned(pair, "seq", 2), turned(pair_forward, "seq", 6)
    gate, w_out = call(
        gate_kernel,
        "gate",
        (out(rows, vw, dtype=F32), pltpu.VMEM(w_out.shape, w_out.dtype)),
        (after(zgate, pair), norm_gain.reshape(1, HEAD), hbm(w_out)),
        4,
        scratch=[pltpu.SemaphoreType.DMA((FETCHES,))],
        inputs=[VMEM, VMEM, ANY],
        specs=(VMEM, ANY),
        cost=10_000_000,
    )
    gate, near, far = lax.optimization_barrier((gate, near, far))
    state = out(half, HEAD, HEAD)
    keep, give = call(enter_kernel, "enter", (state, state), (near, far, mine, other), 4)
    terms = call(
        finish_kernel,
        "finish",
        (out(rows, part),) * groups,
        (base, response, keep, swapped(give, "seq"), gate, vmem(w_out)),
        8,
        scratch=[pltpu.VMEM((rows, vw), BF16), pltpu.VMEM((heads, HEAD, HEAD), BF16)],
    )
    mixed = terms[0].astype(F32)
    for steps in (2, 1, 3):
        mixed = mixed + turned(terms[steps], "head", steps).astype(F32)
    return mixed.astype(BF16)


def solution(mesh):
    return jax.shard_map(
        local,
        mesh=mesh,
        in_specs=(
            P("seq", None),
            P("seq"),
            P(),
            P(None, "head"),
            P(None, "head"),
            P(None, "head"),
            P(None, "head"),
            P(None, "head"),
            P(None, "head"),
            P(None, "head"),
            P(None, "head"),
            P(None, "head"),
            P("head"),
            P("head"),
            P(),
            P("head", None),
        ),
        out_specs=P("seq", "head"),
        check_vma=False,
    )
```

```python
import jax
import jax.numpy as jnp
from jax import lax
from jax.experimental import pallas as pl
from jax.experimental.pallas import tpu as pltpu
from jax.sharding import PartitionSpec as P

HEAD = 128
KERNEL = 4
TAIL = 16
LANES = 128
FETCHES = 4
PACKED = 4
SPOTS = 12
VMEM = pl.BlockSpec(memory_space=pltpu.VMEM)
SMEM = pl.BlockSpec(memory_space=pltpu.SMEM)
ANY = pl.BlockSpec(memory_space=pl.ANY)
F32 = jnp.float32
BF16 = jnp.bfloat16
HIGHEST = lax.Precision.HIGHEST


def iota(shape, axis):
    return lax.broadcasted_iota(jnp.int32, shape, axis)


def dot(left, right, contract=((1,), (0,)), precision=None):
    return lax.dot_general(
        left, right, (contract, ((), ())), precision=precision, preferred_element_type=F32
    )


def params(mib):
    return pltpu.CompilerParams(vmem_limit_bytes=mib << 20)


def pack_kernel(shards, order_ref, tokens_ref, send_ref, part_ref, sem):
    rows, width = part_ref.shape
    slots = send_ref.shape[0]
    capacity = slots // shards
    pieces = width // LANES
    here = pl.multiple_of(lax.axis_index("head") * width, width)
    copy = pltpu.make_async_copy(tokens_ref.at[:, pl.ds(here, width)], part_ref, sem)
    copy.start()
    order = order_ref[...]
    bits = rows.bit_length() - 1
    target = lax.shift_right_logical(order, jnp.full_like(order, bits))
    landing = lax.bitwise_and(order, jnp.full_like(order, rows - 1))
    marks = (iota((shards, rows), 0) == target).astype(F32)
    before = (iota((rows, rows), 0) < iota((rows, rows), 1)).astype(F32).astype(BF16)
    earlier = dot(marks.astype(BF16), before)
    slot = jnp.sum(earlier * marks, axis=0, keepdims=True).astype(jnp.int32)
    spots = jnp.where(iota((LANES, rows), 0) == slot, (landing + 1).astype(F32), 0.0)
    at = iota((slots, rows), 0)

    def chosen(index):
        return (at == index).astype(F32).astype(BF16)

    extra = dot(chosen(target * capacity + SPOTS), spots.astype(BF16), ((1,), (1,)))
    hit = chosen(target * capacity + slot)
    later = jnp.where(target == shards - 1, 0, target + 1) * capacity
    halo = landing - (rows - KERNEL + 1)
    halo = jnp.where(halo >= 0, later + halo * pieces, -pieces)
    halos = [chosen(halo + piece) for piece in range(pieces)]
    copy.wait()
    send_ref[:, :width] = dot(hit, part_ref[...]).astype(BF16)
    for piece in range(pieces):
        extra = extra + dot(halos[piece], part_ref[:, piece * LANES : (piece + 1) * LANES])
    send_ref[:, width:] = extra.astype(BF16)


def place_kernel(shards, got_ref, part_ref):
    slots = got_ref.shape[0]
    width = part_ref.shape[1]
    rows = part_ref.shape[0] - TAIL
    capacity = slots // shards
    pieces = width // LANES
    extra = got_ref[:, width:]
    named = (iota((shards, slots), 1) == iota((shards, slots), 0) * capacity + SPOTS)
    spots = dot(named.astype(F32).astype(BF16), extra).astype(BF16)
    inner = lax.bitwise_and(iota((LANES, slots), 1), capacity - 1)
    turn = (inner == iota((LANES, slots), 0)).astype(F32).astype(BF16)
    outer = iota((shards, slots), 1) - iota((shards, slots), 0) * capacity
    spot = jnp.where((outer >= 0) & (outer < capacity), dot(spots, turn), 0.0)
    spot = jnp.sum(spot, axis=0, keepdims=True).astype(jnp.int32)
    hit = (spot == iota((rows, slots), 0) + 1).astype(F32).astype(BF16)
    part_ref[TAIL:] = dot(hit, got_ref[:, :width]).astype(BF16)
    inner = lax.bitwise_and(iota((TAIL, slots), 1), capacity - 1)
    halo = iota((TAIL, slots), 0) - (TAIL - KERNEL + 1)
    for piece in range(pieces):
        from_slot = (halo >= 0) & (inner == halo * pieces + piece)
        part_ref[:TAIL, piece * LANES : (piece + 1) * LANES] = dot(
            from_slot.astype(F32).astype(BF16), extra
        ).astype(BF16)


def softplus(x):
    return jnp.maximum(x, 0.0) + jnp.log1p(jnp.exp(-jnp.abs(x)))


def in_parts(source, target, sems, first):
    part = source.shape[0] // FETCHES
    return [
        pltpu.make_async_copy(
            source.at[pl.ds(j * part, part)], target.at[pl.ds(j * part, part)], sems.at[first + j]
        )
        for j in range(FETCHES)
    ]


def fetch_kernel(*refs):
    count = (len(refs) - 1) // 2
    copies = []
    for i, (source, target) in enumerate(zip(refs[:count], refs[count : 2 * count])):
        copies += in_parts(source, target, refs[-1], i * FETCHES)
    for copy in copies:
        copy.start()
    for copy in copies:
        copy.wait()


def project_kernel(
    part0_ref,
    part1_ref,
    part2_ref,
    part3_ref,
    w_query,
    w_key,
    w_value,
    w_beta,
    w_alpha,
    decay_log,
    decay_bias,
    balanced_ref,
    query_ref,
    key_ref,
    value_ref,
    beta_ref,
    decay_ref,
):
    parts = (part0_ref, part1_ref, part2_ref, part3_ref)
    width = part0_ref.shape[1]
    here = lax.axis_index("head")
    for steps, part in enumerate(parts):
        at = lax.rem(here + len(parts) - steps, len(parts)) * width
        balanced_ref[:, pl.ds(pl.multiple_of(at, width), width)] = part[...]
    balanced = balanced_ref[...]
    across = ((1,), (1,))
    for weight, to in ((w_query, query_ref), (w_key, key_ref), (w_value, value_ref)):
        for start in range(0, to.shape[1], 512):
            part = dot(balanced, weight[:, start : start + 512])
            to[:, start : start + 512] = part.astype(BF16)
    balanced = balanced_ref[TAIL:]
    beta_ref[...] = jax.nn.sigmoid(dot(balanced, w_beta[...], across))
    decay_ref[...] = -jnp.exp(decay_log[...]) * softplus(
        dot(balanced, w_alpha[...], across) + decay_bias[...]
    )


def project_gate_kernel(balanced_ref, w_zgate, zgate_ref):
    balanced = balanced_ref[TAIL:]
    for start in range(0, zgate_ref.shape[1], 512):
        part = dot(balanced, w_zgate[:, start : start + 512])
        zgate_ref[:, start : start + 512] = part.astype(BF16)


def silu(x):
    return x / (1.0 + jnp.exp(-x))


def document_ends(lengths_ref):
    ends, total = [], jnp.int32(0)
    for i in range(lengths_ref.shape[0]):
        total = total + lengths_ref[i]
        ends.append(total)
    return ends


def segments(position, ends):
    count = (position >= 0).astype(jnp.int32) - 1
    for end in ends:
        count = count + (position >= end).astype(jnp.int32)
    return count


def convolve(projected, taps, same):
    extended = projected.astype(F32)
    sums = None
    for lag in range(KERNEL):
        rolled = extended if lag == 0 else pltpu.roll(extended, lag, 0)
        tap = taps[KERNEL - 1 - lag : KERNEL - lag, :].astype(F32)
        term = rolled[TAIL:] * tap
        if lag:
            term = term * same[lag - 1]
        sums = term if sums is None else sums + term
    return silu(sums)


def unit(x, factor):
    return x * (lax.rsqrt(jnp.sum(x * x, axis=-1, keepdims=True) + 1e-06) * factor)


def masks(first, ends, rows):
    position = first + iota((rows, 1), 0)
    segment = segments(position, ends)
    same = [
        (segments(position - lag, ends) == segment).astype(F32) for lag in range(1, KERNEL)
    ]
    inside = segment == segments(first + iota((1, rows), 1), ends)
    before = segments(jnp.full((1, 1), first - 1, jnp.int32), ends)
    carries = (segment == before).astype(F32)
    return segment, same, inside, carries


def cumulated(decay_ref):
    rows, heads = decay_ref.shape
    lower = (iota((rows, rows), 0) >= iota((rows, rows), 1)).astype(F32)
    down = dot(lower, decay_ref[...], precision=HIGHEST)
    padded = jnp.concatenate([down, jnp.zeros((rows, LANES - heads), F32)], axis=1)
    return down, padded.T


def between(down, across, h, inside):
    difference = down[:, h : h + 1] - across[h : h + 1, :]
    return jnp.where(inside, jnp.exp(jnp.where(inside, difference, 0.0)), 0.0)


def my_core():
    return lax.rem(lax.axis_index("seq"), 2)


def column_of(h):
    return slice(h * HEAD, (h + 1) * HEAD)


def chunk_kernel(
    lengths_ref,
    key_ref,
    value_ref,
    taps_key,
    taps_value,
    beta_ref,
    decay_ref,
    mine_ref,
    send_ref,
    keys,
    solved_ref,
    system_ref,
    packed_ref,
    inverse_ref,
    whole_ref,
    mask_ref,
    states_ref,
    right_ref,
):
    rows = beta_ref.shape[0]
    first, core = lax.axis_index("seq") * rows, my_core()
    heads = beta_ref.shape[1]
    key_heads = key_ref.shape[1] // HEAD
    repeat = heads // key_heads
    width = key_ref.shape[1]
    segment, same, inside, carries = masks(first, document_ends(lengths_ref), rows)
    row, column = iota((rows, rows), 0), iota((rows, rows), 1)
    small = rows // PACKED
    levels = small.bit_length() - 1
    down_row, lane = iota((small, rows), 0), iota((small, rows), 1)
    lane_in = lax.bitwise_and(lane, small - 1)
    for level in range(levels):
        size = 1 << level
        apart = (lax.bitwise_xor(down_row, lane_in) < 2 * size) & (
            lax.bitwise_and(down_row, size) > lax.bitwise_and(lane_in, size)
        )
        mask_ref[level] = apart.astype(F32).astype(BF16)
    diagonal = (down_row == lane_in).astype(F32).astype(BF16)
    blocks = [
        ((lane >= i * small) & (lane < (i + 1) * small)).astype(F32).astype(BF16)
        for i in range(PACKED)
    ]

    def spread(packed):
        return jnp.concatenate([packed * block for block in blocks], axis=0)
    strict = inside & (row > column)
    down, across = cumulated(decay_ref)

    for kh in range(key_heads):
        at = column_of(kh)
        keys[kh] = unit(
            convolve(key_ref[:, at], taps_key[:, at], same), 1.0
        ).astype(BF16)
        inner = dot(keys[kh], keys[kh], ((1,), (1,)))
        for h in range(kh * repeat, (kh + 1) * repeat):
            system = beta_ref[:, h : h + 1] * inner * between(down, across, h, strict)
            system_ref[h] = system.astype(BF16)
    for h in range(heads):
        at = column_of(h)
        beta = beta_ref[:, h : h + 1]
        carried = jnp.exp(down[:, h : h + 1]) * carries
        value = convolve(value_ref[:, at], taps_value[:, at], same)
        right_ref[h, :, :HEAD] = (beta * value).astype(BF16)
        right_ref[h, :, HEAD:] = (beta * carried * keys[h // repeat].astype(F32)).astype(BF16)
    for h in range(heads):
        packed = None
        for i in range(PACKED):
            term = system_ref[h, i * small : (i + 1) * small] * blocks[i]
            packed = term if packed is None else packed + term
        packed_ref[h] = packed
        inverse_ref[h] = diagonal - packed * mask_ref[0]
    for level in range(1, levels):
        for h in range(heads):
            inverse = inverse_ref[h]
            part = dot(packed_ref[h] * mask_ref[level], spread(inverse)).astype(BF16)
            inverse_ref[h] = inverse - dot(inverse, spread(part)).astype(BF16)
    zero = jnp.zeros((small, rows), BF16)
    for h in range(heads):
        inverse = inverse_ref[h]
        spread_inverse = spread(inverse)
        below = (
            system_ref[h, small : 2 * small] * blocks[0]
            + system_ref[h, 3 * small : 4 * small] * blocks[2]
        )
        part = dot(below, spread_inverse).astype(BF16)
        part = jnp.concatenate([zero, part * blocks[0], zero, part * blocks[2]], axis=0)
        part = dot(inverse, part).astype(BF16)
        part = jnp.concatenate([zero, part * blocks[0], zero, part * blocks[2]], axis=0)
        whole_ref[h] = spread_inverse - part

    square = (iota((HEAD, HEAD), 0) == iota((HEAD, HEAD), 1)).astype(F32)
    half, middle = heads // 2, rows // 2
    last_same = (segment == segment[rows - 1 : rows, :]).astype(F32)
    for h in range(heads):
        solved_ref[h, :middle] = dot(
            whole_ref[h, :middle, :middle], right_ref[h, :middle]
        ).astype(BF16)
    for h in range(heads):
        rest = right_ref[h, middle:].astype(F32) - dot(
            system_ref[h, middle:, :middle], solved_ref[h, :middle]
        )
        solved_ref[h, middle:] = dot(whole_ref[h, middle:, middle:], rest.astype(BF16)).astype(
            BF16
        )
    for h in range(heads):
        gain = down[:, h : h + 1]
        last = jnp.exp(gain[rows - 1 : rows, :] - gain) * last_same
        ended = dot((last * keys[h // repeat].astype(F32)).astype(BF16), solved_ref[h], ((0,), (0,)))
        carried = (jnp.exp(gain) * carries)[rows - 1 : rows, :]
        states_ref[0, h] = (carried * square - ended[:, HEAD:]).astype(BF16)
        states_ref[1, h] = ended[:, :HEAD].astype(BF16)

    @pl.when(core == 0)
    def _():
        mine_ref[...] = states_ref[:, :half]
        send_ref[...] = states_ref[:, half:]

    @pl.when(core != 0)
    def _():
        mine_ref[...] = states_ref[:, half:]
        send_ref[...] = states_ref[:, :half]


def chunk_scratch(heads, rows):
    small = rows // PACKED
    return [
        pltpu.VMEM((heads, rows, rows), BF16),
        pltpu.VMEM((heads, small, rows), BF16),
        pltpu.VMEM((heads, small, rows), BF16),
        pltpu.VMEM((heads, rows, rows), BF16),
        pltpu.VMEM((small.bit_length() - 1, small, rows), BF16),
        pltpu.VMEM((2, heads, HEAD, HEAD), BF16),
        pltpu.VMEM((heads, rows, 2 * HEAD), BF16),
    ]


def respond_kernel(
    lengths_ref,
    query_ref,
    taps_query,
    decay_ref,
    keys,
    solved_ref,
    base_ref,
    response_ref,
):
    rows, heads = decay_ref.shape
    key_heads = query_ref.shape[1] // HEAD
    repeat = heads // key_heads
    segment, same, inside, carries = masks(
        lax.axis_index("seq") * rows, document_ends(lengths_ref), rows
    )
    inside = inside & (iota((rows, rows), 0) >= iota((rows, rows), 1))
    down, across = cumulated(decay_ref)
    for kh in range(key_heads):
        at = column_of(kh)
        query = unit(
            convolve(query_ref[:, at], taps_query[:, at], same), HEAD**-0.5
        )
        cross = dot(query.astype(BF16), keys[kh], ((1,), (1,)))
        for h in range(kh * repeat, (kh + 1) * repeat):
            mixing = (between(down, across, h, inside) * cross).astype(BF16)
            mixed = dot(mixing, solved_ref[h])
            carried = jnp.exp(down[:, h : h + 1]) * carries
            base_ref[:, column_of(h)] = mixed[:, :HEAD]
            response_ref[:, column_of(h)] = (carried * query - mixed[:, HEAD:]).astype(BF16)


def gate_kernel(zgate_ref, gain_ref, w_out, gate_ref, out_ref, sems):
    copies = in_parts(w_out, out_ref, sems, 0)
    for copy in copies:
        copy.start()
    for start in range(0, zgate_ref.shape[1], HEAD):
        at = slice(start, start + HEAD)
        gate_ref[:, at] = silu(zgate_ref[:, at].astype(F32)) * gain_ref[...]
    for copy in copies:
        copy.wait()


def chip_kernel(mine_ref, other_ref, chip_ref):
    core = my_core()

    def compose(early, late):
        for h in range(mine_ref.shape[1]):
            left = late[0, h]
            chip_ref[0, h] = dot(left, early[0, h]).astype(BF16)
            chip_ref[1, h] = (dot(left, early[1, h]) + late[1, h].astype(F32)).astype(BF16)

    @pl.when(core == 0)
    def _():
        compose(mine_ref, other_ref)

    @pl.when(core != 0)
    def _():
        compose(other_ref, mine_ref)


def pair_kernel(chip_ref, before_ref, pair_ref, forward_ref):
    for h in range(chip_ref.shape[1]):
        left = chip_ref[0, h]
        pair_ref[0, h] = dot(left, before_ref[0, h]).astype(BF16)
        forward = (dot(left, before_ref[1, h]) + chip_ref[1, h].astype(F32)).astype(BF16)
        pair_ref[1, h] = forward
        forward_ref[h] = forward


def enter_kernel(near_ref, far_ref, mine_ref, other_ref, keep_ref, send_ref):
    core = my_core()

    def step(first_ref, early_ref, late_ref):
        heads = range(far_ref.shape[0])
        for h in heads:
            entering = dot(near_ref[0, h], far_ref[h]) + near_ref[1, h].astype(F32)
            early_ref[h] = entering.astype(BF16)
        for h in heads:
            later = dot(first_ref[0, h], early_ref[h]) + first_ref[1, h].astype(F32)
            late_ref[h] = later.astype(BF16)

    @pl.when(core == 0)
    def _():
        step(mine_ref, keep_ref, send_ref)

    @pl.when(core != 0)
    def _():
        step(other_ref, send_ref, keep_ref)


def finish_kernel(
    base_ref,
    response_ref,
    keep_ref,
    other_ref,
    gate_ref,
    w_out,
    term0_ref,
    term1_ref,
    term2_ref,
    term3_ref,
    gated_ref,
    state_ref,
):
    core = my_core()
    half = keep_ref.shape[0]

    @pl.when(core == 0)
    def _():
        state_ref[:half] = keep_ref[...]
        state_ref[half:] = other_ref[...]

    @pl.when(core != 0)
    def _():
        state_ref[:half] = other_ref[...]
        state_ref[half:] = keep_ref[...]

    for h in range(2 * half):
        at = column_of(h)
        attended = base_ref[:, at] + dot(response_ref[:, at], state_ref[h])
        scale = lax.rsqrt(jnp.mean(attended * attended, axis=-1, keepdims=True) + 1e-06)
        gated_ref[:, at] = (attended * scale * gate_ref[:, at]).astype(BF16)
    gated = gated_ref[...]
    terms = (term0_ref, term1_ref, term2_ref, term3_ref)
    width = term0_ref.shape[1]
    here = lax.axis_index("head")
    for steps, term in enumerate(terms):
        at = pl.multiple_of(lax.rem(here + steps, len(terms)) * width, width)
        term[...] = dot(gated, w_out[:, pl.ds(at, width)]).astype(BF16)


def out(*shape, dtype=BF16):
    return pltpu.VMEM(shape, dtype)


def turned(value, axis, steps):
    count = lax.axis_size(axis)
    return lax.ppermute(value, axis, [(at, (at + steps) % count) for at in range(count)])


def swapped(value, axis):
    count = lax.axis_size(axis)
    return lax.ppermute(value, axis, [(at, at ^ 1) for at in range(count)])


def after(value, *others):
    return lax.optimization_barrier((value, *others))[0]


def hbm(value):
    return pltpu.with_memory_space_constraint(value, pltpu.HBM)


def vmem(value):
    return pltpu.with_memory_space_constraint(value, pltpu.VMEM)


def call(kernel, name, outs, ins, mib, *, scratch=(), cost=2_000_000, inputs=None, specs=None):
    single = not isinstance(outs, tuple)
    outs = (outs,) if single else outs
    got = pl.pallas_call(
        kernel,
        out_shape=outs,
        in_specs=[VMEM] * len(ins) if inputs is None else inputs,
        out_specs=(VMEM,) * len(outs) if specs is None else specs,
        scratch_shapes=list(scratch),
        compiler_params=params(mib),
        cost_estimate=pl.CostEstimate(flops=0, bytes_accessed=cost, transcendentals=0),
        name=name,
    )(*ins)
    return got[0] if single else got


def local(
    tokens,
    order,
    doc_lengths,
    w_query,
    w_key,
    w_value,
    w_zgate,
    w_beta,
    w_alpha,
    conv_query,
    conv_key,
    conv_value,
    decay_log,
    decay_bias,
    norm_gain,
    w_out,
):
    rows, width = tokens.shape
    shards = lax.axis_size("seq")
    groups = lax.axis_size("head")
    capacity = 2 * rows // shards
    slots = shards * capacity
    qk, vw, heads = w_query.shape[1], w_value.shape[1], w_beta.shape[1]
    half, key_heads = heads // 2, qk // HEAD
    part = width // groups

    send = call(
        lambda *refs: pack_kernel(shards, *refs),
        "pack",
        pltpu.HBM((slots, part + LANES), BF16),
        (hbm(order.reshape(1, rows)), hbm(tokens)),
        8,
        scratch=[pltpu.VMEM((rows, part), BF16), pltpu.SemaphoreType.DMA],
        inputs=[VMEM, ANY],
    )
    got = lax.all_to_all(
        send.reshape(shards, capacity, part + LANES), "seq", split_axis=0, concat_axis=0, tiled=True
    ).reshape(slots, part + LANES)
    own = call(
        lambda *refs: place_kernel(shards, *refs), "place", out(TAIL + rows, part), (got,), 4
    )
    parts = [own] + [turned(own, "head", steps) for steps in range(1, groups)]
    weights = [hbm(after(weight, parts[0])) for weight in (w_query, w_key, w_value, w_zgate)]
    fetched = call(
        fetch_kernel,
        "fetch",
        tuple(pltpu.VMEM(weight.shape, weight.dtype) for weight in weights),
        tuple(weights),
        2,
        scratch=[pltpu.SemaphoreType.DMA((FETCHES * len(weights),))],
        inputs=[ANY] * len(weights),
        specs=(ANY,) * len(weights),
        cost=20_000_000,
    )
    balanced, query, key, value, beta, decay = call(
        project_kernel,
        "project",
        (
            out(TAIL + rows, width),
            out(TAIL + rows, qk),
            out(TAIL + rows, qk),
            out(TAIL + rows, vw),
            out(rows, heads, dtype=F32),
            out(rows, heads, dtype=F32),
        ),
        (
            *parts,
            *[vmem(weight) for weight in fetched[:3]],
            w_beta.T,
            w_alpha.T,
            decay_log.reshape(1, heads),
            decay_bias.reshape(1, heads),
        ),
        8,
    )
    states = out(2, half, HEAD, HEAD)
    mine, sent, keys, solved = call(
        chunk_kernel,
        "chunk",
        (states, states, out(key_heads, rows, HEAD), out(heads, rows, 2 * HEAD)),
        (doc_lengths, key, value, conv_key, conv_value, beta, decay),
        16,
        scratch=chunk_scratch(heads, rows),
        inputs=[SMEM] + [VMEM] * 6,
    )
    other = swapped(sent, "seq")
    chip = call(chip_kernel, "chip", states, (mine, other), 4)
    before = turned(chip, "seq", 2)
    base, response = call(
        respond_kernel,
        "respond",
        (out(rows, vw, dtype=F32), out(rows, vw)),
        (doc_lengths, after(query, chip), conv_query, decay, keys, solved),
        8,
        inputs=[SMEM] + [VMEM] * 5,
        cost=16_000_000,
    )
    zgate = call(
        project_gate_kernel,
        "project_gate",
        out(rows, vw),
        (after(balanced, base), vmem(fetched[3])),
        8,
        cost=6_000_000,
    )
    zgate, base, before = lax.optimization_barrier((zgate, base, before))
    pair, pair_forward = call(
        pair_kernel, "pair", (states, out(half, HEAD, HEAD)), (chip, before), 4
    )
    near, far = turned(pair, "seq", 2), turned(pair_forward, "seq", 6)
    gate, w_out = call(
        gate_kernel,
        "gate",
        (out(rows, vw, dtype=F32), pltpu.VMEM(w_out.shape, w_out.dtype)),
        (after(zgate, pair), norm_gain.reshape(1, HEAD), hbm(w_out)),
        4,
        scratch=[pltpu.SemaphoreType.DMA((FETCHES,))],
        inputs=[VMEM, VMEM, ANY],
        specs=(VMEM, ANY),
        cost=10_000_000,
    )
    gate, near, far = lax.optimization_barrier((gate, near, far))
    state = out(half, HEAD, HEAD)
    keep, give = call(enter_kernel, "enter", (state, state), (near, far, mine, other), 4)
    terms = call(
        finish_kernel,
        "finish",
        (out(rows, part),) * groups,
        (base, response, keep, swapped(give, "seq"), gate, vmem(w_out)),
        8,
        scratch=[pltpu.VMEM((rows, vw), BF16), pltpu.VMEM((heads, HEAD, HEAD), BF16)],
    )
    mixed = terms[0].astype(F32)
    for steps in (2, 1, 3):
        mixed = mixed + turned(terms[steps], "head", steps).astype(F32)
    return mixed.astype(BF16)


def solution(mesh):
    return jax.shard_map(
        local,
        mesh=mesh,
        in_specs=(
            P("seq", None),
            P("seq"),
            P(),
            P(None, "head"),
            P(None, "head"),
            P(None, "head"),
            P(None, "head"),
            P(None, "head"),
            P(None, "head"),
            P(None, "head"),
            P(None, "head"),
            P(None, "head"),
            P("head"),
            P("head"),
            P(),
            P("head", None),
        ),
        out_specs=P("seq", "head"),
        check_vma=False,
    )
```

```python
import jax
import jax.numpy as jnp
from jax import lax
from jax.experimental import pallas as pl
from jax.experimental.pallas import tpu as pltpu
from jax.sharding import PartitionSpec as P

HEAD = 128
KERNEL = 4
TAIL = 16
LANES = 128
FETCHES = 4
PACKED = 4
SPOTS = 12
VMEM = pl.BlockSpec(memory_space=pltpu.VMEM)
SMEM = pl.BlockSpec(memory_space=pltpu.SMEM)
ANY = pl.BlockSpec(memory_space=pl.ANY)
F32 = jnp.float32
BF16 = jnp.bfloat16
HIGHEST = lax.Precision.HIGHEST


def iota(shape, axis):
    return lax.broadcasted_iota(jnp.int32, shape, axis)


def dot(left, right, contract=((1,), (0,)), precision=None):
    return lax.dot_general(
        left, right, (contract, ((), ())), precision=precision, preferred_element_type=F32
    )


def params(mib):
    return pltpu.CompilerParams(vmem_limit_bytes=mib << 20)


def pack_kernel(shards, order_ref, tokens_ref, send_ref, part_ref, sem):
    rows, width = part_ref.shape
    slots = send_ref.shape[0]
    capacity = slots // shards
    pieces = width // LANES
    here = pl.multiple_of(lax.axis_index("head") * width, width)
    copy = pltpu.make_async_copy(tokens_ref.at[:, pl.ds(here, width)], part_ref, sem)
    copy.start()
    order = order_ref[...]
    bits = rows.bit_length() - 1
    target = lax.shift_right_logical(order, jnp.full_like(order, bits))
    landing = lax.bitwise_and(order, jnp.full_like(order, rows - 1))
    marks = (iota((shards, rows), 0) == target).astype(F32)
    before = (iota((rows, rows), 0) < iota((rows, rows), 1)).astype(F32).astype(BF16)
    earlier = dot(marks.astype(BF16), before)
    slot = jnp.sum(earlier * marks, axis=0, keepdims=True).astype(jnp.int32)
    spots = jnp.where(iota((LANES, rows), 0) == slot, (landing + 1).astype(F32), 0.0)
    at = iota((slots, rows), 0)

    def chosen(index):
        return (at == index).astype(F32).astype(BF16)

    extra = dot(chosen(target * capacity + SPOTS), spots.astype(BF16), ((1,), (1,)))
    hit = chosen(target * capacity + slot)
    later = jnp.where(target == shards - 1, 0, target + 1) * capacity
    halo = landing - (rows - KERNEL + 1)
    halo = jnp.where(halo >= 0, later + halo * pieces, -pieces)
    halos = [chosen(halo + piece) for piece in range(pieces)]
    copy.wait()
    send_ref[:, :width] = dot(hit, part_ref[...]).astype(BF16)
    for piece in range(pieces):
        extra = extra + dot(halos[piece], part_ref[:, piece * LANES : (piece + 1) * LANES])
    send_ref[:, width:] = extra.astype(BF16)


def place_kernel(shards, got_ref, part_ref):
    slots = got_ref.shape[0]
    width = part_ref.shape[1]
    rows = part_ref.shape[0] - TAIL
    capacity = slots // shards
    pieces = width // LANES
    extra = got_ref[:, width:]
    named = (iota((shards, slots), 1) == iota((shards, slots), 0) * capacity + SPOTS)
    spots = dot(named.astype(F32).astype(BF16), extra).astype(BF16)
    inner = lax.bitwise_and(iota((LANES, slots), 1), capacity - 1)
    turn = (inner == iota((LANES, slots), 0)).astype(F32).astype(BF16)
    outer = iota((shards, slots), 1) - iota((shards, slots), 0) * capacity
    spot = jnp.where((outer >= 0) & (outer < capacity), dot(spots, turn), 0.0)
    spot = jnp.sum(spot, axis=0, keepdims=True).astype(jnp.int32)
    hit = (spot == iota((rows, slots), 0) + 1).astype(F32).astype(BF16)
    part_ref[TAIL:] = dot(hit, got_ref[:, :width]).astype(BF16)
    inner = lax.bitwise_and(iota((TAIL, slots), 1), capacity - 1)
    halo = iota((TAIL, slots), 0) - (TAIL - KERNEL + 1)
    for piece in range(pieces):
        from_slot = (halo >= 0) & (inner == halo * pieces + piece)
        part_ref[:TAIL, piece * LANES : (piece + 1) * LANES] = dot(
            from_slot.astype(F32).astype(BF16), extra
        ).astype(BF16)


def softplus(x):
    return jnp.maximum(x, 0.0) + jnp.log1p(jnp.exp(-jnp.abs(x)))


def in_parts(source, target, sems, first):
    part = source.shape[0] // FETCHES
    return [
        pltpu.make_async_copy(
            source.at[pl.ds(j * part, part)], target.at[pl.ds(j * part, part)], sems.at[first + j]
        )
        for j in range(FETCHES)
    ]


def fetch_kernel(*refs):
    count = (len(refs) - 1) // 2
    copies = []
    for i, (source, target) in enumerate(zip(refs[:count], refs[count : 2 * count])):
        copies += in_parts(source, target, refs[-1], i * FETCHES)
    for copy in copies:
        copy.start()
    for copy in copies:
        copy.wait()


def rows_of(steps, width):
    groups = lax.axis_size("head")
    at = lax.rem(lax.axis_index("head") + groups - steps, groups) * width
    return pl.ds(pl.multiple_of(at, width), width)


ACROSS = ((1,), (1,))


def project_kernel(
    part0_ref,
    part2_ref,
    w_query,
    w_key,
    w_value,
    w_beta,
    w_alpha,
    query_ref,
    key_ref,
    value_ref,
    beta_ref,
    alpha_ref,
):
    width = part0_ref.shape[1]
    parts = [(rows_of(0, width), part0_ref), (rows_of(2, width), part2_ref)]
    for weight, to in ((w_key, key_ref), (w_value, value_ref), (w_query, query_ref)):
        for start in range(0, to.shape[1], 512):
            column = slice(start, start + 512)
            to[:, column] = sum(dot(part[...], weight[at, column]) for at, part in parts)
    for weight, to in ((w_beta, beta_ref), (w_alpha, alpha_ref)):
        to[...] = sum(dot(part[TAIL:], weight[:, at], ACROSS) for at, part in parts)


def project_gate_kernel(part0_ref, part1_ref, part2_ref, part3_ref, w_zgate, zgate_ref):
    width = part0_ref.shape[1]
    parts = [
        (rows_of(n, width), part)
        for n, part in enumerate((part0_ref, part1_ref, part2_ref, part3_ref))
    ]
    for start in range(0, zgate_ref.shape[1], 512):
        column = slice(start, start + 512)
        total = sum(dot(part[TAIL:], w_zgate[at, column]) for at, part in parts)
        zgate_ref[:, column] = total.astype(BF16)


def silu(x):
    return x / (1.0 + jnp.exp(-x))


def document_ends(lengths_ref):
    ends, total = [], jnp.int32(0)
    for i in range(lengths_ref.shape[0]):
        total = total + lengths_ref[i]
        ends.append(total)
    return ends


def segments(position, ends):
    count = (position >= 0).astype(jnp.int32) - 1
    for end in ends:
        count = count + (position >= end).astype(jnp.int32)
    return count


def convolve(projected, taps, same):
    extended = projected.astype(F32)
    sums = None
    for lag in range(KERNEL):
        rolled = extended if lag == 0 else pltpu.roll(extended, lag, 0)
        tap = taps[KERNEL - 1 - lag : KERNEL - lag, :].astype(F32)
        term = rolled[TAIL:] * tap
        if lag:
            term = term * same[lag - 1]
        sums = term if sums is None else sums + term
    return silu(sums)


def unit(x, factor):
    return x * (lax.rsqrt(jnp.sum(x * x, axis=-1, keepdims=True) + 1e-06) * factor)


def masks(first, ends, rows):
    position = first + iota((rows, 1), 0)
    segment = segments(position, ends)
    same = [
        (segments(position - lag, ends) == segment).astype(F32) for lag in range(1, KERNEL)
    ]
    inside = segment == segments(first + iota((1, rows), 1), ends)
    before = segments(jnp.full((1, 1), first - 1, jnp.int32), ends)
    carries = (segment == before).astype(F32)
    return segment, same, inside, carries


def cumulated(decay):
    rows, heads = decay.shape
    lower = (iota((rows, rows), 0) >= iota((rows, rows), 1)).astype(F32)
    down = dot(lower, decay, precision=HIGHEST)
    padded = jnp.concatenate([down, jnp.zeros((rows, LANES - heads), F32)], axis=1)
    return down, padded.T


def between(down, across, h, inside):
    difference = down[:, h : h + 1] - across[h : h + 1, :]
    return jnp.where(inside, jnp.exp(jnp.where(inside, difference, 0.0)), 0.0)


def my_core():
    return lax.rem(lax.axis_index("seq"), 2)


def column_of(h):
    return slice(h * HEAD, (h + 1) * HEAD)


def chunk_kernel(
    lengths_ref,
    part1_ref,
    part3_ref,
    query_sum,
    key_sum,
    value_sum,
    beta_sum,
    alpha_sum,
    w_query,
    w_key,
    w_value,
    w_beta,
    w_alpha,
    decay_log,
    decay_bias,
    taps_key,
    taps_value,
    mine_ref,
    send_ref,
    keys,
    solved_ref,
    query_ref,
    decay_ref,
    key_ref,
    value_ref,
    system_ref,
    packed_ref,
    inverse_ref,
    whole_ref,
    mask_ref,
    states_ref,
    right_ref,
):
    rows, heads = beta_sum.shape
    width = part1_ref.shape[1]
    parts = [(rows_of(1, width), part1_ref), (rows_of(3, width), part3_ref)]

    def project(weight, before, to, start):
        at = slice(start, start + 512)
        total = sum(dot(part[...], weight[own, at]) for own, part in parts)
        to[:, at] = (before[:, at] + total).astype(BF16)

    def small_project(weight, before):
        return before[...] + sum(dot(part[TAIL:], weight[:, own], ACROSS) for own, part in parts)

    beta_all = jax.nn.sigmoid(small_project(w_beta, beta_sum))
    alpha = small_project(w_alpha, alpha_sum)
    decay = -jnp.exp(decay_log[...]) * softplus(alpha + decay_bias[...])
    decay_ref[...] = decay
    project(w_key, key_sum, key_ref, 0)
    fillers = [(w_value, value_sum, value_ref, at) for at in range(0, value_ref.shape[1], 512)]
    fillers += [(w_query, query_sum, query_ref, at) for at in range(0, query_ref.shape[1], 512)]
    first, core = lax.axis_index("seq") * rows, my_core()
    key_heads = key_ref.shape[1] // HEAD
    repeat = heads // key_heads
    segment, same, inside, carries = masks(first, document_ends(lengths_ref), rows)
    row, column = iota((rows, rows), 0), iota((rows, rows), 1)
    small = rows // PACKED
    levels = small.bit_length() - 1
    down_row, lane = iota((small, rows), 0), iota((small, rows), 1)
    lane_in = lax.bitwise_and(lane, small - 1)
    for level in range(levels):
        size = 1 << level
        apart = (lax.bitwise_xor(down_row, lane_in) < 2 * size) & (
            lax.bitwise_and(down_row, size) > lax.bitwise_and(lane_in, size)
        )
        mask_ref[level] = apart.astype(F32).astype(BF16)
    diagonal = (down_row == lane_in).astype(F32).astype(BF16)
    blocks = [
        ((lane >= i * small) & (lane < (i + 1) * small)).astype(F32).astype(BF16)
        for i in range(PACKED)
    ]

    def spread(packed):
        return jnp.concatenate([packed * block for block in blocks], axis=0)
    strict = inside & (row > column)
    down, across = cumulated(decay)

    for kh in range(key_heads):
        at = column_of(kh)
        keys[kh] = unit(
            convolve(key_ref[:, at], taps_key[:, at], same), 1.0
        ).astype(BF16)
        inner = dot(keys[kh], keys[kh], ((1,), (1,)))
        for h in range(kh * repeat, (kh + 1) * repeat):
            system = beta_all[:, h : h + 1] * inner * between(down, across, h, strict)
            system_ref[h] = system.astype(BF16)
    for h in range(heads):
        packed = None
        for i in range(PACKED):
            term = system_ref[h, i * small : (i + 1) * small] * blocks[i]
            packed = term if packed is None else packed + term
        packed_ref[h] = packed
        inverse_ref[h] = diagonal - packed * mask_ref[0]
    for level in range(1, levels):
        if fillers:
            project(*fillers.pop(0))
        for h in range(heads):
            inverse = inverse_ref[h]
            part = dot(packed_ref[h] * mask_ref[level], spread(inverse)).astype(BF16)
            inverse_ref[h] = inverse - dot(inverse, spread(part)).astype(BF16)
    for h in range(heads):
        at = column_of(h)
        beta = beta_all[:, h : h + 1]
        carried = jnp.exp(down[:, h : h + 1]) * carries
        value = convolve(value_ref[:, at], taps_value[:, at], same)
        right_ref[h, :, :HEAD] = (beta * value).astype(BF16)
        right_ref[h, :, HEAD:] = (beta * carried * keys[h // repeat].astype(F32)).astype(BF16)
    zero = jnp.zeros((small, rows), BF16)
    for h in range(heads):
        inverse = inverse_ref[h]
        spread_inverse = spread(inverse)
        below = (
            system_ref[h, small : 2 * small] * blocks[0]
            + system_ref[h, 3 * small : 4 * small] * blocks[2]
        )
        part = dot(below, spread_inverse).astype(BF16)
        part = jnp.concatenate([zero, part * blocks[0], zero, part * blocks[2]], axis=0)
        part = dot(inverse, part).astype(BF16)
        part = jnp.concatenate([zero, part * blocks[0], zero, part * blocks[2]], axis=0)
        whole_ref[h] = spread_inverse - part

    square = (iota((HEAD, HEAD), 0) == iota((HEAD, HEAD), 1)).astype(F32)
    half, middle = heads // 2, rows // 2
    last_same = (segment == segment[rows - 1 : rows, :]).astype(F32)
    for h in range(heads):
        solved_ref[h, :middle] = dot(
            whole_ref[h, :middle, :middle], right_ref[h, :middle]
        ).astype(BF16)
    for h in range(heads):
        rest = right_ref[h, middle:].astype(F32) - dot(
            system_ref[h, middle:, :middle], solved_ref[h, :middle]
        )
        solved_ref[h, middle:] = dot(whole_ref[h, middle:, middle:], rest.astype(BF16)).astype(
            BF16
        )
    for h in range(heads):
        gain = down[:, h : h + 1]
        last = jnp.exp(gain[rows - 1 : rows, :] - gain) * last_same
        ended = dot((last * keys[h // repeat].astype(F32)).astype(BF16), solved_ref[h], ((0,), (0,)))
        carried = (jnp.exp(gain) * carries)[rows - 1 : rows, :]
        states_ref[0, h] = (carried * square - ended[:, HEAD:]).astype(BF16)
        states_ref[1, h] = ended[:, :HEAD].astype(BF16)

    @pl.when(core == 0)
    def _():
        mine_ref[...] = states_ref[:, :half]
        send_ref[...] = states_ref[:, half:]

    @pl.when(core != 0)
    def _():
        mine_ref[...] = states_ref[:, half:]
        send_ref[...] = states_ref[:, :half]


def chunk_scratch(heads, rows, key_width, value_width):
    small = rows // PACKED
    return [
        pltpu.VMEM((TAIL + rows, key_width), BF16),
        pltpu.VMEM((TAIL + rows, value_width), BF16),
        pltpu.VMEM((heads, rows, rows), BF16),
        pltpu.VMEM((heads, small, rows), BF16),
        pltpu.VMEM((heads, small, rows), BF16),
        pltpu.VMEM((heads, rows, rows), BF16),
        pltpu.VMEM((small.bit_length() - 1, small, rows), BF16),
        pltpu.VMEM((2, heads, HEAD, HEAD), BF16),
        pltpu.VMEM((heads, rows, 2 * HEAD), BF16),
    ]


def respond_kernel(
    lengths_ref,
    query_ref,
    taps_query,
    decay_ref,
    keys,
    solved_ref,
    base_ref,
    response_ref,
):
    rows, heads = decay_ref.shape
    key_heads = query_ref.shape[1] // HEAD
    repeat = heads // key_heads
    segment, same, inside, carries = masks(
        lax.axis_index("seq") * rows, document_ends(lengths_ref), rows
    )
    inside = inside & (iota((rows, rows), 0) >= iota((rows, rows), 1))
    down, across = cumulated(decay_ref[...])
    for kh in range(key_heads):
        at = column_of(kh)
        query = unit(
            convolve(query_ref[:, at], taps_query[:, at], same), HEAD**-0.5
        )
        cross = dot(query.astype(BF16), keys[kh], ((1,), (1,)))
        for h in range(kh * repeat, (kh + 1) * repeat):
            mixing = (between(down, across, h, inside) * cross).astype(BF16)
            mixed = dot(mixing, solved_ref[h])
            carried = jnp.exp(down[:, h : h + 1]) * carries
            base_ref[:, column_of(h)] = mixed[:, :HEAD]
            response_ref[:, column_of(h)] = (carried * query - mixed[:, HEAD:]).astype(BF16)


def gate_kernel(zgate_ref, gain_ref, w_out, gate_ref, out_ref, sems):
    copies = in_parts(w_out, out_ref, sems, 0)
    for copy in copies:
        copy.start()
    for start in range(0, zgate_ref.shape[1], HEAD):
        at = slice(start, start + HEAD)
        gate_ref[:, at] = silu(zgate_ref[:, at].astype(F32)) * gain_ref[...]
    for copy in copies:
        copy.wait()


def chip_kernel(mine_ref, other_ref, chip_ref):
    core = my_core()

    def compose(early, late):
        for h in range(mine_ref.shape[1]):
            left = late[0, h]
            chip_ref[0, h] = dot(left, early[0, h]).astype(BF16)
            chip_ref[1, h] = (dot(left, early[1, h]) + late[1, h].astype(F32)).astype(BF16)

    @pl.when(core == 0)
    def _():
        compose(mine_ref, other_ref)

    @pl.when(core != 0)
    def _():
        compose(other_ref, mine_ref)


def pair_kernel(chip_ref, before_ref, pair_ref, forward_ref):
    for h in range(chip_ref.shape[1]):
        left = chip_ref[0, h]
        pair_ref[0, h] = dot(left, before_ref[0, h]).astype(BF16)
        forward = (dot(left, before_ref[1, h]) + chip_ref[1, h].astype(F32)).astype(BF16)
        pair_ref[1, h] = forward
        forward_ref[h] = forward


def enter_kernel(near_ref, far_ref, mine_ref, other_ref, keep_ref, send_ref):
    core = my_core()

    def step(first_ref, early_ref, late_ref):
        heads = range(far_ref.shape[0])
        for h in heads:
            entering = dot(near_ref[0, h], far_ref[h]) + near_ref[1, h].astype(F32)
            early_ref[h] = entering.astype(BF16)
        for h in heads:
            later = dot(first_ref[0, h], early_ref[h]) + first_ref[1, h].astype(F32)
            late_ref[h] = later.astype(BF16)

    @pl.when(core == 0)
    def _():
        step(mine_ref, keep_ref, send_ref)

    @pl.when(core != 0)
    def _():
        step(other_ref, send_ref, keep_ref)


def finish_kernel(
    base_ref,
    response_ref,
    keep_ref,
    other_ref,
    gate_ref,
    w_out,
    term0_ref,
    term1_ref,
    term2_ref,
    term3_ref,
    gated_ref,
    state_ref,
):
    core = my_core()
    half = keep_ref.shape[0]

    @pl.when(core == 0)
    def _():
        state_ref[:half] = keep_ref[...]
        state_ref[half:] = other_ref[...]

    @pl.when(core != 0)
    def _():
        state_ref[:half] = other_ref[...]
        state_ref[half:] = keep_ref[...]

    for h in range(2 * half):
        at = column_of(h)
        attended = base_ref[:, at] + dot(response_ref[:, at], state_ref[h])
        scale = lax.rsqrt(jnp.mean(attended * attended, axis=-1, keepdims=True) + 1e-06)
        gated_ref[:, at] = (attended * scale * gate_ref[:, at]).astype(BF16)
    gated = gated_ref[...]
    terms = (term0_ref, term1_ref, term2_ref, term3_ref)
    width = term0_ref.shape[1]
    here = lax.axis_index("head")
    for steps, term in enumerate(terms):
        at = pl.multiple_of(lax.rem(here + steps, len(terms)) * width, width)
        term[...] = dot(gated, w_out[:, pl.ds(at, width)]).astype(BF16)


def out(*shape, dtype=BF16):
    return pltpu.VMEM(shape, dtype)


def turned(value, axis, steps):
    count = lax.axis_size(axis)
    return lax.ppermute(value, axis, [(at, (at + steps) % count) for at in range(count)])


def swapped(value, axis):
    count = lax.axis_size(axis)
    return lax.ppermute(value, axis, [(at, at ^ 1) for at in range(count)])


def after(value, *others):
    return lax.optimization_barrier((value, *others))[0]


def hbm(value):
    return pltpu.with_memory_space_constraint(value, pltpu.HBM)


def vmem(value):
    return pltpu.with_memory_space_constraint(value, pltpu.VMEM)


def call(kernel, name, outs, ins, mib, *, scratch=(), cost=2_000_000, inputs=None, specs=None):
    single = not isinstance(outs, tuple)
    outs = (outs,) if single else outs
    got = pl.pallas_call(
        kernel,
        out_shape=outs,
        in_specs=[VMEM] * len(ins) if inputs is None else inputs,
        out_specs=(VMEM,) * len(outs) if specs is None else specs,
        scratch_shapes=list(scratch),
        compiler_params=params(mib),
        cost_estimate=pl.CostEstimate(flops=0, bytes_accessed=cost, transcendentals=0),
        name=name,
    )(*ins)
    return got[0] if single else got


def local(
    tokens,
    order,
    doc_lengths,
    w_query,
    w_key,
    w_value,
    w_zgate,
    w_beta,
    w_alpha,
    conv_query,
    conv_key,
    conv_value,
    decay_log,
    decay_bias,
    norm_gain,
    w_out,
):
    rows, width = tokens.shape
    shards = lax.axis_size("seq")
    groups = lax.axis_size("head")
    capacity = 2 * rows // shards
    slots = shards * capacity
    qk, vw, heads = w_query.shape[1], w_value.shape[1], w_beta.shape[1]
    half, key_heads = heads // 2, qk // HEAD
    part = width // groups

    send = call(
        lambda *refs: pack_kernel(shards, *refs),
        "pack",
        pltpu.HBM((slots, part + LANES), BF16),
        (hbm(order.reshape(1, rows)), hbm(tokens)),
        8,
        scratch=[pltpu.VMEM((rows, part), BF16), pltpu.SemaphoreType.DMA],
        inputs=[VMEM, ANY],
    )
    got = lax.all_to_all(
        send.reshape(shards, capacity, part + LANES), "seq", split_axis=0, concat_axis=0, tiled=True
    ).reshape(slots, part + LANES)
    own = call(
        lambda *refs: place_kernel(shards, *refs), "place", out(TAIL + rows, part), (got,), 4
    )
    parts = [own] + [turned(own, "head", steps) for steps in range(1, groups)]
    weights = [hbm(after(weight, parts[0])) for weight in (w_query, w_key, w_value, w_zgate)]
    fetched = call(
        fetch_kernel,
        "fetch",
        tuple(pltpu.VMEM(weight.shape, weight.dtype) for weight in weights),
        tuple(weights),
        2,
        scratch=[pltpu.SemaphoreType.DMA((FETCHES * len(weights),))],
        inputs=[ANY] * len(weights),
        specs=(ANY,) * len(weights),
        cost=20_000_000,
    )
    w_beta, w_alpha = w_beta.T, w_alpha.T
    decay_log, decay_bias = decay_log.reshape(1, heads), decay_bias.reshape(1, heads)
    w_query, w_key, w_value, w_zgate = [vmem(weight) for weight in fetched]
    f32 = lambda *shape: out(*shape, dtype=F32)
    query_sum, key_sum, value_sum, beta_sum, alpha_sum = call(
        project_kernel,
        "project",
        (
            f32(TAIL + rows, qk),
            f32(TAIL + rows, qk),
            f32(TAIL + rows, vw),
            f32(rows, heads),
            f32(rows, heads),
        ),
        (parts[0], parts[2], w_query, w_key, w_value, w_beta, w_alpha),
        8,
        cost=10_000_000,
    )
    key_sum, part1, part3 = lax.optimization_barrier((key_sum, parts[1], parts[3]))
    states = out(2, half, HEAD, HEAD)
    mine, sent, keys, solved, query, decay = call(
        chunk_kernel,
        "chunk",
        (
            states,
            states,
            out(key_heads, rows, HEAD),
            out(heads, rows, 2 * HEAD),
            out(TAIL + rows, qk),
            f32(rows, heads),
        ),
        (
            doc_lengths,
            part1,
            part3,
            query_sum,
            key_sum,
            value_sum,
            beta_sum,
            alpha_sum,
            w_query,
            w_key,
            w_value,
            w_beta,
            w_alpha,
            decay_log,
            decay_bias,
            conv_key,
            conv_value,
        ),
        20,
        scratch=chunk_scratch(heads, rows, qk, vw),
        inputs=[SMEM] + [VMEM] * 16,
    )
    other = swapped(sent, "seq")
    chip = call(chip_kernel, "chip", states, (mine, other), 4)
    before = turned(chip, "seq", 2)
    base, response = call(
        respond_kernel,
        "respond",
        (out(rows, vw, dtype=F32), out(rows, vw)),
        (doc_lengths, after(query, chip), conv_query, decay, keys, solved),
        8,
        inputs=[SMEM] + [VMEM] * 5,
        cost=16_000_000,
    )
    zgate = call(
        project_gate_kernel,
        "project_gate",
        out(rows, vw),
        (after(parts[0], base), *parts[1:], w_zgate),
        8,
        cost=6_000_000,
    )
    zgate, base, before = lax.optimization_barrier((zgate, base, before))
    pair, pair_forward = call(
        pair_kernel, "pair", (states, out(half, HEAD, HEAD)), (chip, before), 4
    )
    near, far = turned(pair, "seq", 2), turned(pair_forward, "seq", 6)
    gate, w_out = call(
        gate_kernel,
        "gate",
        (out(rows, vw, dtype=F32), pltpu.VMEM(w_out.shape, w_out.dtype)),
        (after(zgate, pair), norm_gain.reshape(1, HEAD), hbm(w_out)),
        4,
        scratch=[pltpu.SemaphoreType.DMA((FETCHES,))],
        inputs=[VMEM, VMEM, ANY],
        specs=(VMEM, ANY),
        cost=10_000_000,
    )
    gate, near, far = lax.optimization_barrier((gate, near, far))
    state = out(half, HEAD, HEAD)
    keep, give = call(enter_kernel, "enter", (state, state), (near, far, mine, other), 4)
    terms = call(
        finish_kernel,
        "finish",
        (out(rows, part),) * groups,
        (base, response, keep, swapped(give, "seq"), gate, vmem(w_out)),
        8,
        scratch=[pltpu.VMEM((rows, vw), BF16), pltpu.VMEM((heads, HEAD, HEAD), BF16)],
    )
    mixed = terms[0].astype(F32)
    for steps in (2, 1, 3):
        mixed = mixed + turned(terms[steps], "head", steps).astype(F32)
    return mixed.astype(BF16)


def solution(mesh):
    return jax.shard_map(
        local,
        mesh=mesh,
        in_specs=(
            P("seq", None),
            P("seq"),
            P(),
            P(None, "head"),
            P(None, "head"),
            P(None, "head"),
            P(None, "head"),
            P(None, "head"),
            P(None, "head"),
            P(None, "head"),
            P(None, "head"),
            P(None, "head"),
            P("head"),
            P("head"),
            P(),
            P("head", None),
        ),
        out_specs=P("seq", "head"),
        check_vma=False,
    )
```

```python
import jax
import jax.numpy as jnp
from jax import lax
from jax.experimental import pallas as pl
from jax.experimental.pallas import tpu as pltpu
from jax.sharding import PartitionSpec as P

HEAD = 128
KERNEL = 4
TAIL = 16
LANES = 128
FETCHES = 4
PACKED = 4
SPOTS = 12
VMEM = pl.BlockSpec(memory_space=pltpu.VMEM)
SMEM = pl.BlockSpec(memory_space=pltpu.SMEM)
ANY = pl.BlockSpec(memory_space=pl.ANY)
F32 = jnp.float32
BF16 = jnp.bfloat16


def iota(shape, axis):
    return lax.broadcasted_iota(jnp.int32, shape, axis)


def dot(left, right, contract=((1,), (0,))):
    return lax.dot_general(
        left, right, (contract, ((), ())), preferred_element_type=F32
    )


def params(mib):
    return pltpu.CompilerParams(vmem_limit_bytes=mib << 20)


def pack_kernel(shards, order_ref, tokens_ref, send_ref, part_ref, filled_ref, sem, sems):
    rows, width = part_ref.shape
    slots = send_ref.shape[0]
    capacity = slots // shards
    pieces = width // LANES
    here = pl.multiple_of(lax.axis_index("head") * width, width)
    copy = pltpu.make_async_copy(tokens_ref.at[:, pl.ds(here, width)], part_ref, sem)
    copy.start()
    order = order_ref[...]
    bits = rows.bit_length() - 1
    target = lax.shift_right_logical(order, jnp.full_like(order, bits))
    landing = lax.bitwise_and(order, jnp.full_like(order, rows - 1))
    marks = (iota((shards, rows), 0) == target).astype(F32)
    before = (iota((rows, rows), 0) < iota((rows, rows), 1)).astype(F32).astype(BF16)
    earlier = dot(marks.astype(BF16), before)
    slot = jnp.sum(earlier * marks, axis=0, keepdims=True).astype(jnp.int32)
    spots = jnp.where(iota((LANES, rows), 0) == slot, (landing + 1).astype(F32), 0.0)
    at = iota((slots, rows), 0)

    def chosen(index):
        return (at == index).astype(F32).astype(BF16)

    extra = dot(chosen(target * capacity + SPOTS), spots.astype(BF16), ((1,), (1,)))
    hit = chosen(target * capacity + slot)
    later = jnp.where(target == shards - 1, 0, target + 1) * capacity
    halo = landing - (rows - KERNEL + 1)
    halo = jnp.where(halo >= 0, later + halo * pieces, -pieces)
    halos = [chosen(halo + piece) for piece in range(pieces)]
    copy.wait()
    for piece in range(pieces):
        extra = extra + dot(halos[piece], part_ref[:, piece * LANES : (piece + 1) * LANES])
    filled_ref[:, width:] = extra.astype(BF16)
    block = slots // FETCHES
    copies = in_parts(filled_ref, send_ref, sems, 0)
    for i, copy in enumerate(copies):
        at = slice(i * block, (i + 1) * block)
        filled_ref[at, :width] = dot(hit[at], part_ref[...]).astype(BF16)
        copy.start()
    for copy in copies:
        copy.wait()


def place_kernel(shards, got_ref, part_ref):
    slots = got_ref.shape[0]
    width = part_ref.shape[1]
    rows = part_ref.shape[0] - TAIL
    capacity = slots // shards
    pieces = width // LANES
    extra = got_ref[:, width:]
    named = (iota((shards, slots), 1) == iota((shards, slots), 0) * capacity + SPOTS)
    spots = dot(named.astype(F32).astype(BF16), extra).astype(BF16)
    inner = lax.bitwise_and(iota((LANES, slots), 1), capacity - 1)
    turn = (inner == iota((LANES, slots), 0)).astype(F32).astype(BF16)
    outer = iota((shards, slots), 1) - iota((shards, slots), 0) * capacity
    spot = jnp.where((outer >= 0) & (outer < capacity), dot(spots, turn), 0.0)
    spot = jnp.sum(spot, axis=0, keepdims=True).astype(jnp.int32)
    hit = (spot == iota((rows, slots), 0) + 1).astype(F32).astype(BF16)
    part_ref[TAIL:] = dot(hit, got_ref[:, :width]).astype(BF16)
    inner = lax.bitwise_and(iota((TAIL, slots), 1), capacity - 1)
    halo = iota((TAIL, slots), 0) - (TAIL - KERNEL + 1)
    for piece in range(pieces):
        from_slot = (halo >= 0) & (inner == halo * pieces + piece)
        part_ref[:TAIL, piece * LANES : (piece + 1) * LANES] = dot(
            from_slot.astype(F32).astype(BF16), extra
        ).astype(BF16)


def softplus(x):
    return jnp.maximum(x, 0.0) + jnp.log1p(jnp.exp(-jnp.abs(x)))


def in_parts(source, target, sems, first):
    part = source.shape[0] // FETCHES
    return [
        pltpu.make_async_copy(
            source.at[pl.ds(j * part, part)], target.at[pl.ds(j * part, part)], sems.at[first + j]
        )
        for j in range(FETCHES)
    ]


def fetch_kernel(*refs):
    count = (len(refs) - 1) // 2
    copies = []
    for i, (source, target) in enumerate(zip(refs[:count], refs[count : 2 * count])):
        copies += in_parts(source, target, refs[-1], i * FETCHES)
    for copy in copies:
        copy.start()
    for copy in copies:
        copy.wait()


def rows_of(steps, width):
    groups = lax.axis_size("head")
    at = lax.rem(lax.axis_index("head") + groups - steps, groups) * width
    return pl.ds(pl.multiple_of(at, width), width)


ACROSS = ((1,), (1,))


def project_kernel(
    part0_ref,
    part2_ref,
    w_query,
    w_key,
    w_value,
    w_beta,
    w_alpha,
    query_ref,
    key_ref,
    value_ref,
    beta_ref,
    alpha_ref,
):
    width = part0_ref.shape[1]
    parts = [(rows_of(0, width), part0_ref), (rows_of(2, width), part2_ref)]
    for weight, to in ((w_key, key_ref), (w_value, value_ref), (w_query, query_ref)):
        for start in range(0, to.shape[1], 512):
            column = slice(start, start + 512)
            to[:, column] = sum(dot(part[...], weight[at, column]) for at, part in parts)
    for weight, to in ((w_beta, beta_ref), (w_alpha, alpha_ref)):
        to[...] = sum(dot(part[TAIL:], weight[:, at], ACROSS) for at, part in parts)


def project_gate_kernel(part0_ref, part1_ref, part2_ref, part3_ref, w_zgate, zgate_ref):
    width = part0_ref.shape[1]
    parts = [
        (rows_of(n, width), part)
        for n, part in enumerate((part0_ref, part1_ref, part2_ref, part3_ref))
    ]
    for start in range(0, zgate_ref.shape[1], 512):
        column = slice(start, start + 512)
        total = sum(dot(part[TAIL:], w_zgate[at, column]) for at, part in parts)
        zgate_ref[:, column] = total.astype(BF16)


def silu(x):
    return x / (1.0 + jnp.exp(-x))


def document_ends(lengths_ref):
    ends, total = [], jnp.int32(0)
    for i in range(lengths_ref.shape[0]):
        total = total + lengths_ref[i]
        ends.append(total)
    return ends


def segments(position, ends):
    count = (position >= 0).astype(jnp.int32) - 1
    for end in ends:
        count = count + (position >= end).astype(jnp.int32)
    return count


def convolve(projected, taps, same):
    extended = projected.astype(F32)
    sums = None
    for lag in range(KERNEL):
        rolled = extended if lag == 0 else pltpu.roll(extended, lag, 0)
        tap = taps[KERNEL - 1 - lag : KERNEL - lag, :].astype(F32)
        term = rolled[TAIL:] * tap
        if lag:
            term = term * same[lag - 1]
        sums = term if sums is None else sums + term
    return silu(sums)


def unit(x, factor):
    return x * (lax.rsqrt(jnp.sum(x * x, axis=-1, keepdims=True) + 1e-06) * factor)


def masks(first, ends, rows):
    position = first + iota((rows, 1), 0)
    segment = segments(position, ends)
    same = [
        (segments(position - lag, ends) == segment).astype(F32) for lag in range(1, KERNEL)
    ]
    segment_row = segments(first + iota((1, rows), 1), ends)
    inside = segment == segment_row
    before = segments(jnp.full((1, 1), first - 1, jnp.int32), ends)
    carries = (segment == before).astype(F32)
    return segment_row, same, inside, carries


def cumulated(decay):
    rows, heads = decay.shape
    lower = (iota((rows, rows), 0) >= iota((rows, rows), 1)).astype(F32).astype(BF16)
    high = decay.astype(BF16)
    rest = decay - high.astype(F32)
    middle = rest.astype(BF16)
    low = (rest - middle.astype(F32)).astype(BF16)
    thirds = [part.astype(F32) for part in (high, middle, low)]
    sums = dot(lower, jnp.concatenate(thirds, axis=1).astype(BF16))
    down = sums[:, :heads] + (sums[:, heads : 2 * heads] + sums[:, 2 * heads :])
    padded = jnp.concatenate([down, jnp.zeros((rows, LANES - heads), F32)], axis=1)
    return down, padded.T


def between(down, across, h, inside):
    difference = down[:, h : h + 1] - across[h : h + 1, :]
    return jnp.where(inside, jnp.exp(jnp.where(inside, difference, 0.0)), 0.0)


def my_core():
    return lax.rem(lax.axis_index("seq"), 2)


def column_of(h):
    return slice(h * HEAD, (h + 1) * HEAD)


def chunk_kernel(
    lengths_ref,
    part1_ref,
    part3_ref,
    query_sum,
    key_sum,
    value_sum,
    beta_sum,
    alpha_sum,
    w_query,
    w_key,
    w_value,
    w_beta,
    w_alpha,
    decay_log,
    decay_bias,
    taps_key,
    taps_value,
    mine_ref,
    send_ref,
    keys,
    solved_ref,
    query_ref,
    decay_ref,
    key_ref,
    value_ref,
    system_ref,
    packed_ref,
    inverse_ref,
    whole_ref,
    mask_ref,
    states_ref,
    right_ref,
    part_ref,
    last_ref,
):
    rows, heads = beta_sum.shape
    width = part1_ref.shape[1]
    parts = [(rows_of(1, width), part1_ref), (rows_of(3, width), part3_ref)]

    def project(weight, before, to, start):
        at = slice(start, start + 512)
        total = sum(dot(part[...], weight[own, at]) for own, part in parts)
        to[:, at] = (before[:, at] + total).astype(BF16)

    def small_project(weight, before):
        return before[...] + sum(dot(part[TAIL:], weight[:, own], ACROSS) for own, part in parts)

    beta_all = jax.nn.sigmoid(small_project(w_beta, beta_sum))
    alpha = small_project(w_alpha, alpha_sum)
    decay = -jnp.exp(decay_log[...]) * softplus(alpha + decay_bias[...])
    decay_ref[...] = decay
    project(w_key, key_sum, key_ref, 0)
    fillers = [(w_value, value_sum, value_ref, at) for at in range(0, value_ref.shape[1], 512)]
    fillers += [(w_query, query_sum, query_ref, at) for at in range(0, query_ref.shape[1], 512)]
    first, core = lax.axis_index("seq") * rows, my_core()
    key_heads = key_ref.shape[1] // HEAD
    repeat = heads // key_heads
    segment_row, same, inside, carries = masks(first, document_ends(lengths_ref), rows)
    row, column = iota((rows, rows), 0), iota((rows, rows), 1)
    small = rows // PACKED
    levels = small.bit_length() - 1
    down_row, lane = iota((small, rows), 0), iota((small, rows), 1)
    lane_in = lax.bitwise_and(lane, small - 1)
    for level in range(levels):
        size = 1 << level
        apart = (lax.bitwise_xor(down_row, lane_in) < 2 * size) & (
            lax.bitwise_and(down_row, size) > lax.bitwise_and(lane_in, size)
        )
        mask_ref[level] = apart.astype(F32).astype(BF16)
    diagonal = (down_row == lane_in).astype(F32).astype(BF16)
    blocks = [
        ((lane >= i * small) & (lane < (i + 1) * small)).astype(F32).astype(BF16)
        for i in range(PACKED)
    ]

    def spread(packed):
        return jnp.concatenate([packed * block for block in blocks], axis=0)
    strict = inside & (row > column)
    down, across = cumulated(decay)

    for kh in range(key_heads):
        at = column_of(kh)
        key = unit(convolve(key_ref[:, at], taps_key[:, at], same), 1.0)
        keys[kh] = key.astype(BF16)
    for kh in range(key_heads):
        inner = dot(keys[kh], keys[kh], ((1,), (1,)))
        for h in range(kh * repeat, (kh + 1) * repeat):
            system = beta_all[:, h : h + 1] * inner * between(down, across, h, strict)
            system_ref[h] = system.astype(BF16)
    for h in range(heads):
        packed = None
        for i in range(PACKED):
            term = system_ref[h, i * small : (i + 1) * small] * blocks[i]
            packed = term if packed is None else packed + term
        packed_ref[h] = packed
        inverse_ref[h] = diagonal - packed * mask_ref[0]

    def fill_right(some):
        for h in some:
            at = column_of(h)
            beta = beta_all[:, h : h + 1]
            carried = jnp.exp(down[:, h : h + 1]) * carries
            value = convolve(value_ref[:, at], taps_value[:, at], same)
            right_ref[h, :, :HEAD] = (beta * value).astype(BF16)
            right_ref[h, :, HEAD:] = (beta * carried * keys[h // repeat].astype(F32)).astype(BF16)

    def fill_last():
        for kh in range(key_heads):
            key = keys[kh].astype(F32).T
            for h in range(kh * repeat, (kh + 1) * repeat):
                gain = across[h : h + 1, :]
                last = jnp.where(segment_row == segment_row[:, rows - 1 :], 1.0, 0.0)
                last = jnp.exp(gain[:, rows - 1 :] - gain) * last
                last_ref[h] = (key * last).astype(BF16)

    work = {}
    for level, filler in enumerate(fillers):
        work.setdefault(min(level + 1, levels - 1), []).append(lambda filler=filler: project(*filler))
    for level in range(1, levels):
        for step in work.get(level, []):
            step()
        for h in range(heads):
            inverse = inverse_ref[h]
            part = dot(packed_ref[h] * mask_ref[level], spread(inverse)).astype(BF16)
            inverse_ref[h] = inverse - dot(inverse, spread(part)).astype(BF16)
    zero = jnp.zeros((small, rows), BF16)
    fill_right(range(heads))
    fill_last()
    for h in range(heads):
        inverse = inverse_ref[h]
        spread_inverse = spread(inverse)
        below = (
            system_ref[h, small : 2 * small] * blocks[0]
            + system_ref[h, 3 * small : 4 * small] * blocks[2]
        )
        part = dot(below, spread_inverse).astype(BF16)
        part = jnp.concatenate([zero, part * blocks[0], zero, part * blocks[2]], axis=0)
        part = dot(inverse, part).astype(BF16)
        part = jnp.concatenate([zero, part * blocks[0], zero, part * blocks[2]], axis=0)
        whole_ref[h] = spread_inverse - part

    square = (iota((HEAD, HEAD), 0) == iota((HEAD, HEAD), 1)).astype(F32)
    half, middle = heads // 2, rows // 2
    for h in range(heads):
        solved_ref[h, :middle] = dot(
            whole_ref[h, :middle, :middle], right_ref[h, :middle]
        ).astype(BF16)
    for h in range(heads):
        rest = right_ref[h, middle:].astype(F32) - dot(
            system_ref[h, middle:, :middle], solved_ref[h, :middle]
        )
        right_ref[h, middle:] = rest.astype(BF16)
    for h in range(heads):
        solved_ref[h, middle:] = dot(
            whole_ref[h, middle:, middle:], right_ref[h, middle:]
        ).astype(BF16)
    for h in range(heads):
        ended = dot(last_ref[h], solved_ref[h])
        carried = (jnp.exp(down[:, h : h + 1]) * carries)[rows - 1 : rows, :]
        states_ref[0, h] = (carried * square - ended[:, HEAD:]).astype(BF16)
        states_ref[1, h] = ended[:, :HEAD].astype(BF16)

    @pl.when(core == 0)
    def _():
        mine_ref[...] = states_ref[:, :half]
        send_ref[...] = states_ref[:, half:]

    @pl.when(core != 0)
    def _():
        mine_ref[...] = states_ref[:, half:]
        send_ref[...] = states_ref[:, :half]


def chunk_scratch(heads, rows, key_width, value_width):
    small = rows // PACKED
    return [
        pltpu.VMEM((TAIL + rows, key_width), BF16),
        pltpu.VMEM((TAIL + rows, value_width), BF16),
        pltpu.VMEM((heads, rows, rows), BF16),
        pltpu.VMEM((heads, small, rows), BF16),
        pltpu.VMEM((heads, small, rows), BF16),
        pltpu.VMEM((heads, rows, rows), BF16),
        pltpu.VMEM((small.bit_length() - 1, small, rows), BF16),
        pltpu.VMEM((2, heads, HEAD, HEAD), BF16),
        pltpu.VMEM((heads, rows, 2 * HEAD), BF16),
        pltpu.VMEM((heads, small, rows), BF16),
        pltpu.VMEM((heads, HEAD, rows), BF16),
    ]


def respond_kernel(
    lengths_ref,
    query_ref,
    taps_query,
    decay_ref,
    keys,
    solved_ref,
    base_ref,
    response_ref,
):
    rows, heads = decay_ref.shape
    key_heads = query_ref.shape[1] // HEAD
    repeat = heads // key_heads
    _, same, inside, carries = masks(
        lax.axis_index("seq") * rows, document_ends(lengths_ref), rows
    )
    inside = inside & (iota((rows, rows), 0) >= iota((rows, rows), 1))
    down, across = cumulated(decay_ref[...])
    for kh in range(key_heads):
        at = column_of(kh)
        query = unit(
            convolve(query_ref[:, at], taps_query[:, at], same), HEAD**-0.5
        )
        cross = dot(query.astype(BF16), keys[kh], ((1,), (1,)))
        for h in range(kh * repeat, (kh + 1) * repeat):
            mixing = (between(down, across, h, inside) * cross).astype(BF16)
            mixed = dot(mixing, solved_ref[h])
            carried = jnp.exp(down[:, h : h + 1]) * carries
            base_ref[:, column_of(h)] = mixed[:, :HEAD]
            response_ref[:, column_of(h)] = (carried * query - mixed[:, HEAD:]).astype(BF16)


def gate_kernel(zgate_ref, gain_ref, w_out, gate_ref, out_ref, sems):
    copies = in_parts(w_out, out_ref, sems, 0)
    for copy in copies:
        copy.start()
    for start in range(0, zgate_ref.shape[1], HEAD):
        at = slice(start, start + HEAD)
        gate_ref[:, at] = silu(zgate_ref[:, at].astype(F32)) * gain_ref[...]
    for copy in copies:
        copy.wait()


def chip_kernel(mine_ref, other_ref, chip_ref):
    core = my_core()

    def compose(early, late):
        for h in range(mine_ref.shape[1]):
            left = late[0, h]
            chip_ref[0, h] = dot(left, early[0, h]).astype(BF16)
            chip_ref[1, h] = (dot(left, early[1, h]) + late[1, h].astype(F32)).astype(BF16)

    @pl.when(core == 0)
    def _():
        compose(mine_ref, other_ref)

    @pl.when(core != 0)
    def _():
        compose(other_ref, mine_ref)


def pair_kernel(chip_ref, before_ref, pair_ref, forward_ref):
    for h in range(chip_ref.shape[1]):
        left = chip_ref[0, h]
        pair_ref[0, h] = dot(left, before_ref[0, h]).astype(BF16)
        forward = (dot(left, before_ref[1, h]) + chip_ref[1, h].astype(F32)).astype(BF16)
        pair_ref[1, h] = forward
        forward_ref[h] = forward


def enter_kernel(near_ref, far_ref, mine_ref, other_ref, keep_ref, send_ref):
    core = my_core()

    def step(first_ref, early_ref, late_ref):
        heads = range(far_ref.shape[0])
        for h in heads:
            entering = dot(near_ref[0, h], far_ref[h]) + near_ref[1, h].astype(F32)
            early_ref[h] = entering.astype(BF16)
        for h in heads:
            later = dot(first_ref[0, h], early_ref[h]) + first_ref[1, h].astype(F32)
            late_ref[h] = later.astype(BF16)

    @pl.when(core == 0)
    def _():
        step(mine_ref, keep_ref, send_ref)

    @pl.when(core != 0)
    def _():
        step(other_ref, send_ref, keep_ref)


def finish_kernel(
    base_ref,
    response_ref,
    keep_ref,
    other_ref,
    gate_ref,
    w_out,
    term0_ref,
    term1_ref,
    term2_ref,
    term3_ref,
    gated_ref,
    state_ref,
):
    core = my_core()
    half = keep_ref.shape[0]

    @pl.when(core == 0)
    def _():
        state_ref[:half] = keep_ref[...]
        state_ref[half:] = other_ref[...]

    @pl.when(core != 0)
    def _():
        state_ref[:half] = other_ref[...]
        state_ref[half:] = keep_ref[...]

    for h in range(2 * half):
        at = column_of(h)
        attended = base_ref[:, at] + dot(response_ref[:, at], state_ref[h])
        scale = lax.rsqrt(jnp.mean(attended * attended, axis=-1, keepdims=True) + 1e-06)
        gated_ref[:, at] = (attended * scale * gate_ref[:, at]).astype(BF16)
    gated = gated_ref[...]
    terms = (term0_ref, term1_ref, term2_ref, term3_ref)
    width = term0_ref.shape[1]
    here = lax.axis_index("head")
    for steps, term in enumerate(terms):
        at = pl.multiple_of(lax.rem(here + steps, len(terms)) * width, width)
        term[...] = dot(gated, w_out[:, pl.ds(at, width)]).astype(BF16)


def out(*shape, dtype=BF16):
    return pltpu.VMEM(shape, dtype)


def turned(value, axis, steps):
    count = lax.axis_size(axis)
    return lax.ppermute(value, axis, [(at, (at + steps) % count) for at in range(count)])


def swapped(value, axis):
    count = lax.axis_size(axis)
    return lax.ppermute(value, axis, [(at, at ^ 1) for at in range(count)])


def after(value, *others):
    return lax.optimization_barrier((value, *others))[0]


def hbm(value):
    return pltpu.with_memory_space_constraint(value, pltpu.HBM)


def vmem(value):
    return pltpu.with_memory_space_constraint(value, pltpu.VMEM)


def call(kernel, name, outs, ins, mib, *, scratch=(), cost=2_000_000, inputs=None, specs=None):
    single = not isinstance(outs, tuple)
    outs = (outs,) if single else outs
    got = pl.pallas_call(
        kernel,
        out_shape=outs,
        in_specs=[VMEM] * len(ins) if inputs is None else inputs,
        out_specs=(VMEM,) * len(outs) if specs is None else specs,
        scratch_shapes=list(scratch),
        compiler_params=params(mib),
        cost_estimate=pl.CostEstimate(flops=0, bytes_accessed=cost, transcendentals=0),
        name=name,
    )(*ins)
    return got[0] if single else got


def local(
    tokens,
    order,
    doc_lengths,
    w_query,
    w_key,
    w_value,
    w_zgate,
    w_beta,
    w_alpha,
    conv_query,
    conv_key,
    conv_value,
    decay_log,
    decay_bias,
    norm_gain,
    w_out,
):
    rows, width = tokens.shape
    shards = lax.axis_size("seq")
    groups = lax.axis_size("head")
    capacity = 2 * rows // shards
    slots = shards * capacity
    qk, vw, heads = w_query.shape[1], w_value.shape[1], w_beta.shape[1]
    half, key_heads = heads // 2, qk // HEAD
    part = width // groups

    send = call(
        lambda *refs: pack_kernel(shards, *refs),
        "pack",
        pltpu.HBM((slots, part + LANES), BF16),
        (hbm(order.reshape(1, rows)), hbm(tokens)),
        8,
        scratch=[
            pltpu.VMEM((rows, part), BF16),
            pltpu.VMEM((slots, part + LANES), BF16),
            pltpu.SemaphoreType.DMA,
            pltpu.SemaphoreType.DMA((FETCHES,)),
        ],
        inputs=[VMEM, ANY],
        specs=(ANY,),
    )
    got = lax.all_to_all(
        send.reshape(shards, capacity, part + LANES), "seq", split_axis=0, concat_axis=0, tiled=True
    ).reshape(slots, part + LANES)
    own = call(
        lambda *refs: place_kernel(shards, *refs), "place", out(TAIL + rows, part), (got,), 4
    )
    parts = [own] + [turned(own, "head", steps) for steps in range(1, groups)]
    weights = [hbm(after(weight, parts[0])) for weight in (w_query, w_key, w_value, w_zgate)]
    fetched = call(
        fetch_kernel,
        "fetch",
        tuple(pltpu.VMEM(weight.shape, weight.dtype) for weight in weights),
        tuple(weights),
        2,
        scratch=[pltpu.SemaphoreType.DMA((FETCHES * len(weights),))],
        inputs=[ANY] * len(weights),
        specs=(ANY,) * len(weights),
        cost=20_000_000,
    )
    w_beta, w_alpha = w_beta.T, w_alpha.T
    decay_log, decay_bias = decay_log.reshape(1, heads), decay_bias.reshape(1, heads)
    w_query, w_key, w_value, w_zgate = [vmem(weight) for weight in fetched]
    f32 = lambda *shape: out(*shape, dtype=F32)
    query_sum, key_sum, value_sum, beta_sum, alpha_sum = call(
        project_kernel,
        "project",
        (
            f32(TAIL + rows, qk),
            f32(TAIL + rows, qk),
            f32(TAIL + rows, vw),
            f32(rows, heads),
            f32(rows, heads),
        ),
        (parts[0], parts[2], w_query, w_key, w_value, w_beta, w_alpha),
        8,
        cost=10_000_000,
    )
    key_sum, part1, part3 = lax.optimization_barrier((key_sum, parts[1], parts[3]))
    states = out(2, half, HEAD, HEAD)
    mine, sent, keys, solved, query, decay = call(
        chunk_kernel,
        "chunk",
        (
            states,
            states,
            out(key_heads, rows, HEAD),
            out(heads, rows, 2 * HEAD),
            out(TAIL + rows, qk),
            f32(rows, heads),
        ),
        (
            doc_lengths,
            part1,
            part3,
            query_sum,
            key_sum,
            value_sum,
            beta_sum,
            alpha_sum,
            w_query,
            w_key,
            w_value,
            w_beta,
            w_alpha,
            decay_log,
            decay_bias,
            conv_key,
            conv_value,
        ),
        20,
        scratch=chunk_scratch(heads, rows, qk, vw),
        inputs=[SMEM] + [VMEM] * 16,
    )
    other = swapped(sent, "seq")
    chip = call(chip_kernel, "chip", states, (mine, other), 4)
    before = turned(chip, "seq", 2)
    base, response = call(
        respond_kernel,
        "respond",
        (out(rows, vw, dtype=F32), out(rows, vw)),
        (doc_lengths, after(query, chip), conv_query, decay, keys, solved),
        8,
        inputs=[SMEM] + [VMEM] * 5,
        cost=16_000_000,
    )
    zgate = call(
        project_gate_kernel,
        "project_gate",
        out(rows, vw),
        (after(parts[0], base), *parts[1:], w_zgate),
        8,
        cost=6_000_000,
    )
    zgate, base, before = lax.optimization_barrier((zgate, base, before))
    pair, pair_forward = call(
        pair_kernel, "pair", (states, out(half, HEAD, HEAD)), (chip, before), 4
    )
    near, far = turned(pair, "seq", 2), turned(pair_forward, "seq", 6)
    gate, w_out = call(
        gate_kernel,
        "gate",
        (out(rows, vw, dtype=F32), pltpu.VMEM(w_out.shape, w_out.dtype)),
        (after(zgate, pair), norm_gain.reshape(1, HEAD), hbm(w_out)),
        4,
        scratch=[pltpu.SemaphoreType.DMA((FETCHES,))],
        inputs=[VMEM, VMEM, ANY],
        specs=(VMEM, ANY),
        cost=10_000_000,
    )
    gate, near, far = lax.optimization_barrier((gate, near, far))
    state = out(half, HEAD, HEAD)
    keep, give = call(enter_kernel, "enter", (state, state), (near, far, mine, other), 4)
    terms = call(
        finish_kernel,
        "finish",
        (out(rows, part),) * groups,
        (base, response, keep, swapped(give, "seq"), gate, vmem(w_out)),
        8,
        scratch=[pltpu.VMEM((rows, vw), BF16), pltpu.VMEM((heads, HEAD, HEAD), BF16)],
    )
    mixed = terms[0].astype(F32)
    for steps in (1, 3, 2):
        mixed = mixed + turned(terms[steps], "head", steps).astype(F32)
    return mixed.astype(BF16)


def solution(mesh):
    return jax.shard_map(
        local,
        mesh=mesh,
        in_specs=(
            P("seq", None),
            P("seq"),
            P(),
            P(None, "head"),
            P(None, "head"),
            P(None, "head"),
            P(None, "head"),
            P(None, "head"),
            P(None, "head"),
            P(None, "head"),
            P(None, "head"),
            P(None, "head"),
            P("head"),
            P("head"),
            P(),
            P("head", None),
        ),
        out_specs=P("seq", "head"),
        check_vma=False,
    )
```
